32 devices in a mesh: fsdp: 8 (over z, y), tp: 4 (over x, core).
Axes of the slice: x: 2, y: 2, z: 4, core: 2. Of those that a mesh axis runs over, the one named last changes fastest.
Arguments:
- dout: bfloat16 [2048, 4096], P('fsdp', 'tp'), may hold values from -6 to 6
- w_out: bfloat16 [8192, 4096], P(('tp', 'fsdp')), may hold values from -0.09375 to 0.09375
- y_scan: bfloat16 [2048, 8192], P('fsdp', 'tp'), may hold values from -6 to 6
- z_gate: bfloat16 [2048, 8192], P('fsdp', 'tp'), may hold values from -6 to 6
- x_conv: bfloat16 [2048, 8192], P('fsdp', 'tp'), may hold values from -6 to 6
- du_scan: bfloat16 [2048, 8192], P('fsdp', 'tp'), may hold values from -9 to 9
- conv_w: float32 [4, 8192], P(None, 'tp'), may hold values from -3 to 3
- conv_b: float32 [8192], P('tp'), may hold values from -1 to 1
Outputs:
- d_y: bfloat16 [2048, 8192], P('fsdp', 'tp')
- d_z: bfloat16 [2048, 8192], P('fsdp', 'tp')
- d_x: bfloat16 [2048, 8192], P('fsdp', 'tp')
- d_conv_w: float32 [4, 8192], P(None, 'tp')
- d_conv_b: float32 [8192], P('tp')
The draws below stay inside these ranges and needn't reach their ends.
All inputs are finite; a program needn't handle non-finite values.
Results may differ from the reference program's by a relative error of at most 0.001.
Values may be sent and summed in bfloat16 or wider, within the bound.
A program may use at most 64 MiB of HBM per device.

```python
import jax
import jax.numpy as jnp
from jax import lax

D = 4096
E = 8192
KW = 4
TOK_DEV = 256
TOKENS = 2048
N_TP = 4


def draw_du_scan(key, part):
    position = jnp.arange(TOKENS, dtype=jnp.float32) / (TOKENS - 1)
    ramp = 0.5 + position
    values = jax.random.normal(key, (TOKENS, E), jnp.float32) * ramp[:, None]
    return jnp.clip(values, -9.0, 9.0).astype(jnp.bfloat16)


def shard_levels(stream_key, dims, shards, low, largest):
    factor_of = 1.0
    for dim, blocks in shards:
        draws = jax.random.uniform(jax.random.fold_in(jax.random.fold_in(stream_key, 6), dim), (blocks,), jnp.float32, low / len(shards), largest / len(shards))
        factor_of = factor_of * jnp.repeat(jnp.exp(draws), dims[dim] // blocks).reshape((-1,) + (1,) * (len(dims) - 1 - dim))
    return factor_of


def noise(stream_key, shape, deviation, limit, shards=(), held_as=jnp.bfloat16):
    entries = deviation * jax.random.normal(stream_key, shape, jnp.float32)
    if shards:
        entries = entries * shard_levels(stream_key, shape, shards, -0.22, 0.18)
    return jnp.clip(entries, -limit, limit).astype(held_as)


def setup_inputs(seed: int = 0) -> dict:
    keys = jax.random.split(jax.random.key(seed), 9)
    return {
        "dout": noise(keys[0], (TOKENS, D), 1.0, 6.0, ((0, 8), (1, 4))),
        "w_out": noise(keys[1], (E, D), D ** -0.5, 0.09375, ((0, 32),)),
        "y_scan": noise(keys[2], (TOKENS, E), 1.0, 6.0, ((0, 8), (1, 4))),
        "z_gate": noise(keys[3], (TOKENS, E), 1.0, 6.0, ((0, 8), (1, 4))),
        "x_conv": noise(keys[4], (TOKENS, E), 1.0, 6.0, ((0, 8), (1, 4))),
        "du_scan": draw_du_scan(jax.random.fold_in(keys[8], 71), 0),
        "conv_w": noise(keys[6], (KW, E), 0.5, 3.0, ((1, 4),), jnp.float32),
        "conv_b": jnp.clip(jax.random.uniform(keys[7], (E,), jnp.float32, -1.0, 1.0) * shard_levels(keys[7], (E,), ((0, 4),), -0.4, 0.0), -1.0, 1.0),
    }


def silu_slope(value):
    sig = jax.nn.sigmoid(value)
    return sig * (1.0 + value * (1.0 - sig))


def reference(dout, w_out, y_scan, z_gate, x_conv, du_scan, conv_w, conv_b):
    nblk = TOKENS // TOK_DEV

    def outer(block):
        d_blk, y_blk, z_blk = block
        d_gated = jnp.dot(d_blk, w_out.T, preferred_element_type=jnp.float32)
        zf = z_blk.astype(jnp.float32)
        grad_y = (d_gated * jax.nn.silu(zf)).astype(jnp.bfloat16)
        grad_z = (d_gated * y_blk.astype(jnp.float32) * silu_slope(zf)).astype(jnp.bfloat16)
        return grad_y, grad_z

    grad_y, grad_z = lax.map(outer, (dout.reshape(nblk, TOK_DEV, D), y_scan.reshape(nblk, TOK_DEV, E), z_gate.reshape(nblk, TOK_DEV, E)))
    grad_y = grad_y.reshape(TOKENS, E)
    grad_z = grad_z.reshape(TOKENS, E)

    width = E // N_TP
    nchan = E // width

    def conv_block(block):
        xb, ub, wb, bb = block
        xpad = jnp.concatenate([jnp.zeros((KW - 1, width), jnp.float32), xb.astype(jnp.float32)], 0)
        pre = jnp.zeros((TOKENS, width), jnp.float32) + bb[None, :]
        for k in range(KW):
            pre = pre + wb[k][None, :] * xpad[k:k + TOKENS]
        d_pre = ub.astype(jnp.float32) * silu_slope(pre)
        dpad = jnp.concatenate([d_pre, jnp.zeros((KW - 1, width), jnp.float32)], 0)
        grad_x = jnp.zeros((TOKENS, width), jnp.float32)
        taps = []
        for k in range(KW):
            grad_x = grad_x + wb[k][None, :] * dpad[KW - 1 - k:KW - 1 - k + TOKENS]
            taps.append(jnp.sum(d_pre * xpad[k:k + TOKENS], 0))
        return grad_x.astype(jnp.bfloat16), jnp.stack(taps), jnp.sum(d_pre, 0)

    xs = x_conv.reshape(TOKENS, nchan, width).transpose(1, 0, 2)
    us = du_scan.reshape(TOKENS, nchan, width).transpose(1, 0, 2)
    ws = conv_w.reshape(KW, nchan, width).transpose(1, 0, 2)
    bs = conv_b.reshape(nchan, width)
    grad_x, grad_w, grad_b = lax.map(conv_block, (xs, us, ws, bs))
    grad_x = grad_x.transpose(1, 0, 2).reshape(TOKENS, E)
    grad_w = grad_w.transpose(1, 0, 2).reshape(KW, E)
    grad_b = grad_b.reshape(E)
    return (grad_y, grad_z, grad_x, grad_w, grad_b)
```

```python
import functools

import jax
import jax.numpy as jnp
from jax import lax
from jax.experimental import pallas as pl
from jax.experimental.pallas import tpu as pltpu
from jax.sharding import PartitionSpec as P

KW = 4
HALO = 16
MESH = pl.DeviceIdType.MESH
F32 = jnp.float32
BF16 = jnp.bfloat16


def silu_slope(value):
    sig = jax.nn.sigmoid(value)
    return sig * (1.0 + value * (1.0 - sig))


def kernel(
    nf, nt, dout, w, y_in, z_in, x_in, du_in, cw, cb,
    oy, oz, ox, owb,
    dbuf, wo, wn, sbuf, rbuf, xb, ub, yb, zb, hp, hl, xe, ue, pe, tb, tr, tg,
    lsem, dr, zs, xs, cs, ws, wr, ss, rr, hs, hr, ts, trs, gs, gr,
):
    nz = nf // 2
    f = lax.axis_index("fsdp")
    t = lax.axis_index("tp")
    z, y = lax.div(f, 2), lax.rem(f, 2)
    x, c = lax.div(t, 2), lax.rem(t, 2)
    yf = z * 2 + 1 - y
    tx = (1 - x) * 2 + c
    tc = x * 2 + 1 - c
    tok, depth = dout.shape
    rows = w.shape[0]
    half = rows // 2

    def remote(src, dst, send, recv, fi, ti):
        return pltpu.make_async_remote_copy(
            src_ref=src, dst_ref=dst, send_sem=send, recv_sem=recv, device_id=(fi, ti), device_id_type=MESH
        )

    loads = [
        pltpu.make_async_copy(dout, dbuf.at[z, t], lsem.at[0]),
        pltpu.make_async_copy(x_in, xb, lsem.at[1]),
        pltpu.make_async_copy(du_in, ub, lsem.at[2]),
        pltpu.make_async_copy(w, wo, lsem.at[3]),
        pltpu.make_async_copy(y_in, yb, lsem.at[4]),
        pltpu.make_async_copy(z_in, zb, lsem.at[5]),
    ]
    for one in loads:
        one.start()

    barrier = pltpu.get_barrier_semaphore()
    for o in range(1, nf):
        pl.semaphore_signal(barrier, inc=1, device_id=(lax.rem(f + o, nf), t), device_id_type=MESH)
    pl.semaphore_signal(barrier, inc=1, device_id=(f, tx), device_id_type=MESH)
    pl.semaphore_signal(barrier, inc=1, device_id=(f, tc), device_id_type=MESH)
    pl.semaphore_wait(barrier, nf + 1)

    def halo_next():
        return remote(x_in.at[pl.ds(tok - HALO, HALO)], hp, hs.at[0], hr.at[0], f + 1, t)

    def halo_prev(i):
        src = (x_in, du_in)[i]
        return remote(src.at[pl.ds(0, HALO)], hl.at[i], hs.at[1 + i], hr.at[1 + i], f - 1, t)

    @pl.when(f < nf - 1)
    def _():
        halo_next().start()

    @pl.when(f > 0)
    def _():
        halo_prev(0).start()
        halo_prev(1).start()

    def copy_z(zz, sgn):
        return remote(dbuf.at[zz, t], dbuf.at[zz, t], zs.at[zz, (sgn + 1) // 2], dr.at[zz, t], (z + sgn) * 2 + y, t)

    def copy_x(zz):
        return remote(dbuf.at[zz, t], dbuf.at[zz, t], xs.at[zz], dr.at[zz, t], f, tx)

    def copy_c(zz, which):
        tt = (t, tx)[which]
        return remote(dbuf.at[zz, tt], dbuf.at[zz, tt], cs.at[zz, which], dr.at[zz, tt], f, tc)

    def arrived(zz, tt):
        remote(dbuf.at[zz, tt], dbuf.at[zz, tt], cs.at[zz, 0], dr.at[zz, tt], f, tc).wait_recv()

    def copy_w(h):
        return remote(w.at[pl.ds(h * half, half)], wn.at[h], ws.at[h], wr.at[h], yf, t)

    def valid(i):
        return (i >= 0) & (i < nz)

    def around(s, do):
        for sgn in (1, -1):
            zz = z + sgn * s

            @pl.when(valid(zz))
            def _():
                do(zz, sgn)

    loads[0].wait()
    for sgn in (1, -1):

        @pl.when(valid(z + sgn))
        def _():
            copy_z(z, sgn).start()

    copy_x(z).start()
    copy_c(z, 0).start()
    for h in range(2):
        copy_w(h).start()

    @pl.when(f == 0)
    def _():
        hp[...] = jnp.zeros_like(hp)

    @pl.when(f == nf - 1)
    def _():
        hl[...] = jnp.zeros_like(hl)

    loads[1].wait()
    loads[2].wait()

    @pl.when(f > 0)
    def _():
        halo_next().wait_recv()

    @pl.when(f < nf - 1)
    def _():
        halo_prev(0).wait_recv()
        halo_prev(1).wait_recv()

    wide = tb.shape[2]

    def columns(j):
        return pl.ds(pl.multiple_of(j * wide, wide), wide)

    def conv(j, carry):
        cols = columns(j)
        xe[0:8] = hp[:, cols].astype(F32)[8:16]
        xe[8 : 8 + tok] = xb[:, cols].astype(F32)
        xe[8 + tok : 16 + tok] = hl[0, :, cols].astype(F32)[0:8]
        ue[0:tok] = ub[:, cols].astype(F32)
        ue[tok : tok + 8] = hl[1, :, cols].astype(F32)[0:8]
        taps = cw[:, cols]
        pre = cb[:, cols] + jnp.zeros((tok + 8, wide), F32)
        for k in range(KW):
            pre = pre + taps[k : k + 1] * xe[5 + k : 5 + k + tok + 8]
        pe[...] = ue[...] * silu_slope(pre)
        grad_x = jnp.zeros((tok, wide), F32)
        d_pre = pe[0:tok]
        sums = []
        for k in range(KW):
            grad_x = grad_x + taps[k : k + 1] * pe[KW - 1 - k : KW - 1 - k + tok]
            sums.append(jnp.sum(d_pre * xe[5 + k : 5 + k + tok], 0, keepdims=True))
        sums.append(jnp.sum(d_pre, 0, keepdims=True))
        ox[:, cols] = grad_x.astype(BF16)
        tb[j] = jnp.concatenate(sums + [jnp.zeros((3, wide), F32)], 0)
        return carry

    lax.fori_loop(0, nf, conv, 0)

    def tap_out(o):
        to = lax.rem(f + o, nf)
        return remote(tb.at[to], tr.at[f], ts.at[o], trs.at[f], to, t)

    def tap_in(o):
        at = lax.rem(f + o, nf)
        return remote(tb.at[at], tr.at[at], ts.at[o], trs.at[at], at, t)

    def sum_out(o):
        return remote(tg.at[f], tg.at[f], gs.at[o], gr.at[f], lax.rem(f + o, nf), t)

    def sum_in(o):
        at = lax.rem(f + o, nf)
        return remote(tg.at[at], tg.at[at], gs.at[o], gr.at[at], at, t)

    for o in range(1, nf):
        tap_out(o).start()

    part = depth

    def result_own(zz):
        return remote(sbuf.at[zz, pl.ds(0, 2)], rbuf.at[f], ss.at[zz, 0], rr.at[f, 0], zz * 2 + y, t)

    def result_near(zz, h):
        return remote(sbuf.at[zz, 2 + h], rbuf.at[yf, h], ss.at[zz, 1 + h], rr.at[yf, h], zz * 2 + y, t)

    def product(zz, weights, width):
        total = jnp.zeros((tok, width), F32)
        for k in range(nt):
            total = total + lax.dot_general(
                dbuf[zz, k], weights[:, k * part : (k + 1) * part], (((1,), (1,)), ((), ())),
                preferred_element_type=F32,
            )
        return total

    def comp_own(zz):
        total = product(zz, wo, rows)
        sbuf[zz, 0] = total[:, :half]
        sbuf[zz, 1] = total[:, half:]

    def forward(s):
        def do(zz, sgn):
            arrived(zz, t)

            @pl.when(valid(z - sgn))
            def _():
                copy_z(zz, -sgn).start()

            copy_x(zz).start()
            copy_c(zz, 0).start()

        around(s, do)

    def cross(zz, sgn=0):
        arrived(zz, tx)
        copy_c(zz, 1).start()

    def whole(zz):
        arrived(zz, tc)
        arrived(zz, (1 - x) * 2 + 1 - c)

    def own_around(s):
        def step(i, carry):
            zz = z + (1 - 2 * i) * s

            @pl.when(valid(zz))
            def _():
                whole(zz)
                comp_own(zz)
                result_own(zz).start()

            return carry

        lax.fori_loop(0, 2, step, 0)

    forward(1)
    cross(z)
    whole(z)
    loads[3].wait()
    comp_own(z)
    for s in range(2, nz):
        forward(s)
        around(s - 1, cross)
        own_around(s - 1)
        if s == 2:
            total = tb[f]
            for o in range(1, nf):
                tap_in(o).wait_recv()
                total = total + tr[lax.rem(f + o, nf)]
            tg[f] = total
            for o in range(1, nf):
                sum_out(o).start()
    around(nz - 1, cross)
    own_around(nz - 1)

    for h in range(2):
        copy_w(h).wait_recv()

        def near(i, carry):
            zz = z + (1 - 2 * lax.rem(i, 2)) * lax.div(i + 2, 2)

            @pl.when(valid(zz))
            def _():
                sbuf[zz, 2 + h] = product(zz, wn.at[h], half)
                result_near(zz, h).start()

            return carry

        lax.fori_loop(0, 2 * (nz - 1), near, 0)
        sbuf[z, 2 + h] = product(z, wn.at[h], half)

    loads[4].wait()
    loads[5].wait()

    def gate(values, at):
        cols = pl.ds(pl.multiple_of(at, half), half)
        gate_f = zb[:, cols].astype(F32)
        sig = jax.nn.sigmoid(gate_f)
        oy[:, cols] = (values * (gate_f * sig)).astype(BF16)
        slope = sig * (1.0 + gate_f * (1.0 - sig))
        oz[:, cols] = (values * yb[:, cols].astype(F32) * slope).astype(BF16)

    for q in range(2):
        gate(sbuf[z, q], f * rows + q * half)
        gate(sbuf[z, 2 + q], yf * rows + q * half)

    def finish_own(i, carry):
        zz = z + (1 - 2 * lax.rem(i, 2)) * lax.div(i + 2, 2)

        @pl.when(valid(zz))
        def _():
            fi = zz * 2 + y
            remote(sbuf.at[zz, pl.ds(0, 2)], rbuf.at[fi], ss.at[zz, 0], rr.at[fi, 0], fi, t).wait_recv()
            for q in range(2):
                gate(rbuf[fi, q], fi * rows + q * half)

        return carry

    lax.fori_loop(0, 2 * (nz - 1), finish_own, 0)
    for h in range(2):

        def finish_near(i, carry):
            zz = z + (1 - 2 * lax.rem(i, 2)) * lax.div(i + 2, 2)

            @pl.when(valid(zz))
            def _():
                fi = zz * 2 + 1 - y
                remote(sbuf.at[zz, 2 + h], rbuf.at[fi, h], ss.at[zz, 1 + h], rr.at[fi, h], zz * 2 + y, t).wait_recv()
                gate(rbuf[fi, h], fi * rows + h * half)

            return carry

        lax.fori_loop(0, 2 * (nz - 1), finish_near, 0)

    for o in range(1, nf):
        sum_in(o).wait_recv()
    for j in range(nf):
        owb[:, j * wide : (j + 1) * wide] = tg[j]
    for o in range(1, nf):
        tap_out(o).wait_send()
        sum_out(o).wait_send()

    @pl.when(f < nf - 1)
    def _():
        halo_next().wait_send()

    @pl.when(f > 0)
    def _():
        halo_prev(0).wait_send()
        halo_prev(1).wait_send()

    for h in range(2):
        copy_w(h).wait_send()
    for sgn in (1, -1):

        @pl.when(valid(z + sgn))
        def _():
            copy_z(z, sgn).wait_send()

    def sent(zz):
        copy_x(zz).wait_send()
        copy_c(zz, 0).wait_send()
        copy_c(zz, 1).wait_send()

    def drain(zz, sgn):
        @pl.when(valid(z - sgn))
        def _():
            copy_z(zz, -sgn).wait_send()

        sent(zz)
        result_own(zz).wait_send()
        for h in range(2):
            result_near(zz, h).wait_send()

    sent(z)
    for s in range(1, nz):
        around(s, drain)


def fused(nf, nt, dout, w_out, y_scan, z_gate, x_conv, du_scan, conv_w, conv_b):
    tok, depth = dout.shape
    rows = w_out.shape[0]
    width = x_conv.shape[1]
    nz = nf // 2
    wide = width // nf
    anywhere = pl.BlockSpec(memory_space=pl.ANY)
    vmem = pl.BlockSpec(memory_space=pltpu.VMEM)
    dma = pltpu.SemaphoreType.DMA
    grad_y, grad_z, grad_x, sums = pl.pallas_call(
        functools.partial(kernel, nf, nt),
        out_shape=[jax.ShapeDtypeStruct((tok, width), BF16)] * 3 + [jax.ShapeDtypeStruct((8, width), F32)],
        in_specs=[anywhere] * 6 + [vmem] * 2,
        out_specs=[vmem] * 4,
        scratch_shapes=[
            pltpu.VMEM((nz, nt, tok, depth), BF16),
            pltpu.VMEM((rows, nt * depth), BF16),
            pltpu.VMEM((2, rows // 2, nt * depth), BF16),
            pltpu.VMEM((nz, 4, tok, rows // 2), F32),
            pltpu.VMEM((nf, 2, tok, rows // 2), F32),
            pltpu.VMEM((tok, width), BF16),
            pltpu.VMEM((tok, width), BF16),
            pltpu.VMEM((tok, width), BF16),
            pltpu.VMEM((tok, width), BF16),
            pltpu.VMEM((HALO, width), BF16),
            pltpu.VMEM((2, HALO, width), BF16),
            pltpu.VMEM((tok + 16, wide), F32),
            pltpu.VMEM((tok + 8, wide), F32),
            pltpu.VMEM((tok + 8, wide), F32),
            pltpu.VMEM((nf, 8, wide), F32),
            pltpu.VMEM((nf, 8, wide), F32),
            pltpu.VMEM((nf, 8, wide), F32),
            dma((6,)),
            dma((nz, nt)),
            dma((nz, 2)),
            dma((nz,)),
            dma((nz, 2)),
            dma((2,)),
            dma((2,)),
            dma((nz, 3)),
            dma((nf, 2)),
            dma((3,)),
            dma((3,)),
            dma((nf,)),
            dma((nf,)),
            dma((nf,)),
            dma((nf,)),
        ],
        compiler_params=pltpu.CompilerParams(
            collective_id=0, has_side_effects=True, vmem_limit_bytes=48 * 1024 * 1024
        ),
    )(dout, w_out, y_scan, z_gate, x_conv, du_scan, conv_w, conv_b[None, :])
    return grad_y, grad_z, grad_x, sums[:KW], sums[KW]


def shifted(block, axis, distance):
    devices = range(lax.axis_size(axis))
    route = [(i - distance, i) for i in devices if i - distance in devices]
    return lax.ppermute(block, axis, route)


def gathered(dout, w_out, y_scan, z_gate, x_conv, du_scan, conv_w, conv_b):
    tok_rows = x_conv.shape[0]
    width = x_conv.shape[1]
    prior = shifted(x_conv[tok_rows - (KW - 1) :], "fsdp", 1)
    leading = jnp.stack([x_conv[: KW - 1], du_scan[: KW - 1]])
    later = shifted(leading, "fsdp", -1)
    extended = jnp.concatenate([prior, x_conv, later[0]], 0)
    span = tok_rows + KW - 1
    pre_all = jnp.zeros((span, width), F32) + conv_b[None, :]
    for k in range(KW):
        pre_all = pre_all + conv_w[k][None, :] * extended[k : k + span]
    arriving = jnp.concatenate([du_scan, later[1]], 0)
    d_pre_all = arriving.astype(F32) * silu_slope(pre_all)
    d_pre = d_pre_all[:tok_rows]
    grad_x = jnp.zeros((tok_rows, width), F32)
    taps = []
    for k in range(KW):
        grad_x = grad_x + conv_w[k][None, :] * d_pre_all[KW - 1 - k : KW - 1 - k + tok_rows]
        taps.append(jnp.sum(d_pre * extended[k : k + tok_rows], 0))
    grad_w, grad_b = lax.psum((jnp.stack(taps), jnp.sum(d_pre, 0)), "fsdp")
    full_out = lax.all_gather(dout, "tp", axis=1, tiled=True)
    group_w = lax.all_gather(w_out, "fsdp", axis=0, tiled=True)
    d_gated = lax.dot_general(
        full_out, group_w, (((1,), (1,)), ((), ())), preferred_element_type=F32
    )
    gate_f = z_gate.astype(F32)
    grad_y = (d_gated * jax.nn.silu(gate_f)).astype(BF16)
    grad_z = (d_gated * y_scan.astype(F32) * silu_slope(gate_f)).astype(BF16)
    return (grad_y, grad_z, grad_x.astype(BF16), grad_w, grad_b)


def solution(mesh):
    nf, nt = mesh.shape["fsdp"], mesh.shape["tp"]

    def local(dout, w_out, *rest):
        rows = w_out.shape[0]
        kept = nf // 2 * nt * dout.size * 2
        fits = nt == 4 and nf % 2 == 0 and nf >= 6 and rows % 256 == 0 and kept <= 16 * 1024 * 1024
        body = functools.partial(fused, nf, nt) if fits else gathered
        return body(dout, w_out, *rest)

    return jax.shard_map(
        local,
        mesh=mesh,
        in_specs=(
            P("fsdp", "tp"),
            P(("tp", "fsdp"), None),
            P("fsdp", "tp"),
            P("fsdp", "tp"),
            P("fsdp", "tp"),
            P("fsdp", "tp"),
            P(None, "tp"),
            P("tp"),
        ),
        out_specs=(P("fsdp", "tp"), P("fsdp", "tp"), P("fsdp", "tp"), P(None, "tp"), P("tp")),
        check_vma=False,
    )
```

```python
import functools

import jax
import jax.numpy as jnp
from jax import lax
from jax.experimental import pallas as pl
from jax.experimental.pallas import tpu as pltpu
from jax.sharding import PartitionSpec as P

KW = 4
HALO = 16
MESH = pl.DeviceIdType.MESH
F32 = jnp.float32
BF16 = jnp.bfloat16


def silu_slope(value):
    sig = jax.nn.sigmoid(value)
    return sig * (1.0 + value * (1.0 - sig))


def kernel(
    nf, nt, dout, w, y_in, z_in, x_in, du_in, cw, cb,
    oy, oz, ox, owb,
    dbuf, wo, wn, sbuf, rbuf, xb, ub, yb, zb, hp, hl, xe, ue, pe, tb, tr, tg,
    lsem, dr, zs, xs, cs, ws, wr, ss, rr, hs, hr, ts, trs, gs, gr,
):
    nz = nf // 2
    f = lax.axis_index("fsdp")
    t = lax.axis_index("tp")
    z, y = lax.div(f, 2), lax.rem(f, 2)
    x, c = lax.div(t, 2), lax.rem(t, 2)
    yf = z * 2 + 1 - y
    tx = (1 - x) * 2 + c
    tc = x * 2 + 1 - c
    tok, depth = dout.shape
    rows = w.shape[0]
    half = rows // 2
    few = tok // 2

    def remote(src, dst, send, recv, fi, ti):
        return pltpu.make_async_remote_copy(
            src_ref=src, dst_ref=dst, send_sem=send, recv_sem=recv, device_id=(fi, ti), device_id_type=MESH
        )

    loads = [
        pltpu.make_async_copy(dout.at[pl.ds(0, few)], dbuf.at[z, t, 0], lsem.at[0]),
        pltpu.make_async_copy(dout.at[pl.ds(few, few)], dbuf.at[z, t, 1], lsem.at[6]),
        pltpu.make_async_copy(x_in, xb, lsem.at[1]),
        pltpu.make_async_copy(du_in, ub, lsem.at[2]),
        pltpu.make_async_copy(w, wo, lsem.at[3]),
        pltpu.make_async_copy(y_in, yb, lsem.at[4]),
        pltpu.make_async_copy(z_in, zb, lsem.at[5]),
    ]
    for one in loads:
        one.start()

    barrier = pltpu.get_barrier_semaphore()
    for o in range(1, nf):
        pl.semaphore_signal(barrier, inc=1, device_id=(lax.rem(f + o, nf), t), device_id_type=MESH)
    pl.semaphore_signal(barrier, inc=1, device_id=(f, tx), device_id_type=MESH)
    pl.semaphore_signal(barrier, inc=1, device_id=(f, tc), device_id_type=MESH)
    pl.semaphore_wait(barrier, nf + 1)

    def halo_next():
        return remote(x_in.at[pl.ds(tok - HALO, HALO)], hp, hs.at[0], hr.at[0], f + 1, t)

    def halo_prev(i):
        src = (x_in, du_in)[i]
        return remote(src.at[pl.ds(0, HALO)], hl.at[i], hs.at[1 + i], hr.at[1 + i], f - 1, t)

    @pl.when(f < nf - 1)
    def _():
        halo_next().start()

    @pl.when(f > 0)
    def _():
        halo_prev(0).start()
        halo_prev(1).start()

    def copy_z(zz, h, sgn):
        at = dbuf.at[zz, t, h]
        return remote(at, at, zs.at[zz, h, (sgn + 1) // 2], dr.at[zz, t, h], (z + sgn) * 2 + y, t)

    def copy_x(zz, h):
        at = dbuf.at[zz, t, h]
        return remote(at, at, xs.at[zz, h], dr.at[zz, t, h], f, tx)

    def copy_c(zz, h, which):
        tt = (t, tx)[which]
        at = dbuf.at[zz, tt, h]
        return remote(at, at, cs.at[zz, h, which], dr.at[zz, tt, h], f, tc)

    def arrived(zz, tt, h):
        at = dbuf.at[zz, tt, h]
        remote(at, at, cs.at[zz, h, 0], dr.at[zz, tt, h], f, tc).wait_recv()

    def copy_w(h):
        return remote(w.at[pl.ds(h * half, half)], wn.at[h], ws.at[h], wr.at[h], yf, t)

    def valid(i):
        return (i >= 0) & (i < nz)

    def around(s, do):
        for sgn in (1, -1):
            zz = z + sgn * s

            @pl.when(valid(zz))
            def _():
                do(zz, sgn)

    for h in range(2):
        loads[h].wait()
        for sgn in (1, -1):

            @pl.when(valid(z + sgn))
            def _():
                copy_z(z, h, sgn).start()

        copy_c(z, h, 0).start()
    copy_x(z, 0).start()
    for h in range(2):
        copy_w(h).start()

    @pl.when(f == 0)
    def _():
        hp[...] = jnp.zeros_like(hp)

    @pl.when(f == nf - 1)
    def _():
        hl[...] = jnp.zeros_like(hl)

    loads[2].wait()
    loads[3].wait()

    @pl.when(f > 0)
    def _():
        halo_next().wait_recv()

    @pl.when(f < nf - 1)
    def _():
        halo_prev(0).wait_recv()
        halo_prev(1).wait_recv()

    wide = tb.shape[2]

    def columns(j):
        return pl.ds(pl.multiple_of(j * wide, wide), wide)

    def conv(j, carry):
        cols = columns(j)
        xe[0:8] = hp[:, cols].astype(F32)[8:16]
        xe[8 : 8 + tok] = xb[:, cols].astype(F32)
        xe[8 + tok : 16 + tok] = hl[0, :, cols].astype(F32)[0:8]
        ue[0:tok] = ub[:, cols].astype(F32)
        ue[tok : tok + 8] = hl[1, :, cols].astype(F32)[0:8]
        taps = cw[:, cols]
        pre = cb[:, cols] + jnp.zeros((tok + 8, wide), F32)
        for k in range(KW):
            pre = pre + taps[k : k + 1] * xe[5 + k : 5 + k + tok + 8]
        pe[...] = ue[...] * silu_slope(pre)
        grad_x = jnp.zeros((tok, wide), F32)
        d_pre = pe[0:tok]
        sums = []
        for k in range(KW):
            grad_x = grad_x + taps[k : k + 1] * pe[KW - 1 - k : KW - 1 - k + tok]
            sums.append(jnp.sum(d_pre * xe[5 + k : 5 + k + tok], 0, keepdims=True))
        sums.append(jnp.sum(d_pre, 0, keepdims=True))
        ox[:, cols] = grad_x.astype(BF16)
        tb[j] = jnp.concatenate(sums + [jnp.zeros((3, wide), F32)], 0)
        return carry

    first = nf // 2
    lax.fori_loop(0, first, conv, 0)

    def tap_out(o):
        to = lax.rem(f + o, nf)
        return remote(tb.at[to], tr.at[f], ts.at[o], trs.at[f], to, t)

    def tap_in(o):
        at = lax.rem(f + o, nf)
        return remote(tb.at[at], tr.at[at], ts.at[o], trs.at[at], at, t)

    def sum_out(o):
        return remote(tg.at[f], tg.at[f], gs.at[o], gr.at[f], lax.rem(f + o, nf), t)

    def sum_in(o):
        at = lax.rem(f + o, nf)
        return remote(tg.at[at], tg.at[at], gs.at[o], gr.at[at], at, t)

    part = depth

    def result_own(zz, h):
        return remote(sbuf.at[zz, h, pl.ds(0, 2)], rbuf.at[f, h], ss.at[zz, h], rr.at[f, h], zz * 2 + y, t)

    def result_near(zz, q):
        return remote(sbuf.at[zz, :, 2 + q], rbuf.at[yf, :, q], ss.at[zz, 2 + q], rr.at[yf, q], zz * 2 + y, t)

    def dot(a, b):
        return lax.dot_general(a, b, (((1,), (1,)), ((), ())), preferred_element_type=F32)

    def comp_own(zz, h):
        total = jnp.zeros((few, rows), F32)
        for k in range(nt):
            total = total + dot(dbuf[zz, k, h], wo[:, k * part : (k + 1) * part])
        sbuf[zz, h, 0] = total[:, :half]
        sbuf[zz, h, 1] = total[:, half:]

    def comp_near(zz, q):
        total = jnp.zeros((tok, half), F32)
        for k in range(nt):
            total = total + dot(dbuf[zz, k].reshape(tok, part), wn[q, :, k * part : (k + 1) * part])
        sbuf[zz, 0, 2 + q] = total[:few]
        sbuf[zz, 1, 2 + q] = total[few:]

    def forward(s, h):
        def do(zz, sgn):
            arrived(zz, t, h)

            @pl.when(valid(z - sgn))
            def _():
                copy_z(zz, h, -sgn).start()

            copy_x(zz, h).start()
            copy_c(zz, h, 0).start()

        around(s, do)

    def cross(s, h):
        def do(zz, sgn):
            arrived(zz, tx, h)
            copy_c(zz, h, 1).start()

        around(s, do) if s else do(z, 0)

    def whole(zz, h):
        arrived(zz, tc, h)
        arrived(zz, (1 - x) * 2 + 1 - c, h)

    def own_around(s, h):
        def step(i, carry):
            zz = z + (1 - 2 * i) * s

            @pl.when(valid(zz))
            def _():
                whole(zz, h)
                comp_own(zz, h)
                result_own(zz, h).start()

            return carry

        lax.fori_loop(0, 2, step, 0)

    def near_around(s, q):
        def step(i, carry):
            zz = z + (1 - 2 * i) * s

            @pl.when(valid(zz))
            def _():
                comp_near(zz, q)
                result_near(zz, q).start()

            return carry

        lax.fori_loop(0, 2, step, 0)

    def own_here(h):
        whole(z, h)
        comp_own(z, h)

    def share_taps():
        for o in range(1, nf):
            tap_out(o).start()

    def total_taps():
        total = tb[f]
        for o in range(1, nf):
            tap_in(o).wait_recv()
            total = total + tr[lax.rem(f + o, nf)]
        tg[f] = total
        for o in range(1, nf):
            sum_out(o).start()

    stages = [(s, h) for s in range(1, nz) for h in range(2)]
    last = len(stages)
    for i in range(last + 2):
        if i < last:
            forward(*stages[i])
        if i == 0:
            cross(0, 0)
        elif i <= last:
            cross(*stages[i - 1])
        if i == 1:
            copy_x(z, 1).start()
            lax.fori_loop(first, nf, conv, 0)
            share_taps()
        if i >= 2:
            if i == 2:
                loads[4].wait()
            own_around(*stages[i - 2])
        if i == 3:
            cross(0, 1)
            total_taps()
        if i == last - 1:
            copy_w(0).wait_recv()
            near_around(1, 0)
        if i == last:
            near_around(2, 0)
    own_here(0)
    own_here(1)
    for s in range(3, nz):
        near_around(s, 0)
    copy_w(1).wait_recv()
    for s in range(1, nz):
        near_around(s, 1)
    for q in range(2):
        comp_near(z, q)

    loads[5].wait()
    loads[6].wait()

    def gate(values, h, at):
        here = pl.ds(h * few, few)
        cols = pl.ds(pl.multiple_of(at, half), half)
        gate_f = zb[here, cols].astype(F32)
        sig = jax.nn.sigmoid(gate_f)
        oy[here, cols] = (values * (gate_f * sig)).astype(BF16)
        slope = sig * (1.0 + gate_f * (1.0 - sig))
        oz[here, cols] = (values * yb[here, cols].astype(F32) * slope).astype(BF16)

    for h in range(2):
        for q in range(2):
            gate(sbuf[z, h, q], h, f * rows + q * half)
            gate(sbuf[z, h, 2 + q], h, yf * rows + q * half)

    def finish(n, near):
        def step(i, carry):
            zz = z + (1 - 2 * lax.rem(i, 2)) * lax.div(i + 2, 2)

            @pl.when(valid(zz))
            def _():
                fi = zz * 2 + (1 - y if near else y)
                into = rbuf.at[fi, :, n] if near else rbuf.at[fi, n]
                remote(into, into, ss.at[zz, n], rr.at[fi, n], zz * 2 + y, t).wait_recv()
                for m in range(2):
                    h, q = (m, n) if near else (n, m)
                    gate(rbuf[fi, h, q], h, fi * rows + q * half)

            return carry

        lax.fori_loop(0, 2 * (nz - 1), step, 0)

    for near in (False, True):
        for n in range(2):
            finish(n, near)

    for o in range(1, nf):
        sum_in(o).wait_recv()
    for j in range(nf):
        owb[:, j * wide : (j + 1) * wide] = tg[j]
    for o in range(1, nf):
        tap_out(o).wait_send()
        sum_out(o).wait_send()

    @pl.when(f < nf - 1)
    def _():
        halo_next().wait_send()

    @pl.when(f > 0)
    def _():
        halo_prev(0).wait_send()
        halo_prev(1).wait_send()

    for h in range(2):
        copy_w(h).wait_send()
    for h in range(2):
        for sgn in (1, -1):

            @pl.when(valid(z + sgn))
            def _():
                copy_z(z, h, sgn).wait_send()

    def sent(zz):
        for h in range(2):
            copy_x(zz, h).wait_send()
            copy_c(zz, h, 0).wait_send()
            copy_c(zz, h, 1).wait_send()

    def drain(zz, sgn):
        for h in range(2):

            @pl.when(valid(z - sgn))
            def _():
                copy_z(zz, h, -sgn).wait_send()

            result_own(zz, h).wait_send()
            result_near(zz, h).wait_send()

        sent(zz)

    sent(z)
    for s in range(1, nz):
        around(s, drain)


def fused(nf, nt, dout, w_out, y_scan, z_gate, x_conv, du_scan, conv_w, conv_b):
    tok, depth = dout.shape
    rows = w_out.shape[0]
    width = x_conv.shape[1]
    nz = nf // 2
    wide = width // nf
    anywhere = pl.BlockSpec(memory_space=pl.ANY)
    vmem = pl.BlockSpec(memory_space=pltpu.VMEM)
    dma = pltpu.SemaphoreType.DMA
    grad_y, grad_z, grad_x, sums = pl.pallas_call(
        functools.partial(kernel, nf, nt),
        out_shape=[jax.ShapeDtypeStruct((tok, width), BF16)] * 3 + [jax.ShapeDtypeStruct((8, width), F32)],
        in_specs=[anywhere] * 6 + [vmem] * 2,
        out_specs=[vmem] * 4,
        scratch_shapes=[
            pltpu.VMEM((nz, nt, 2, tok // 2, depth), BF16),
            pltpu.VMEM((rows, nt * depth), BF16),
            pltpu.VMEM((2, rows // 2, nt * depth), BF16),
            pltpu.VMEM((nz, 2, 4, tok // 2, rows // 2), F32),
            pltpu.VMEM((nf, 2, 2, tok // 2, rows // 2), F32),
            pltpu.VMEM((tok, width), BF16),
            pltpu.VMEM((tok, width), BF16),
            pltpu.VMEM((tok, width), BF16),
            pltpu.VMEM((tok, width), BF16),
            pltpu.VMEM((HALO, width), BF16),
            pltpu.VMEM((2, HALO, width), BF16),
            pltpu.VMEM((tok + 16, wide), F32),
            pltpu.VMEM((tok + 8, wide), F32),
            pltpu.VMEM((tok + 8, wide), F32),
            pltpu.VMEM((nf, 8, wide), F32),
            pltpu.VMEM((nf, 8, wide), F32),
            pltpu.VMEM((nf, 8, wide), F32),
            dma((7,)),
            dma((nz, nt, 2)),
            dma((nz, 2, 2)),
            dma((nz, 2)),
            dma((nz, 2, 2)),
            dma((2,)),
            dma((2,)),
            dma((nz, 4)),
            dma((nf, 2)),
            dma((3,)),
            dma((3,)),
            dma((nf,)),
            dma((nf,)),
            dma((nf,)),
            dma((nf,)),
        ],
        compiler_params=pltpu.CompilerParams(
            collective_id=0, has_side_effects=True, vmem_limit_bytes=60 * 1024 * 1024
        ),
    )(dout, w_out, y_scan, z_gate, x_conv, du_scan, conv_w, conv_b[None, :])
    return grad_y, grad_z, grad_x, sums[:KW], sums[KW]


def shifted(block, axis, distance):
    devices = range(lax.axis_size(axis))
    route = [(i - distance, i) for i in devices if i - distance in devices]
    return lax.ppermute(block, axis, route)


def gathered(dout, w_out, y_scan, z_gate, x_conv, du_scan, conv_w, conv_b):
    tok_rows = x_conv.shape[0]
    width = x_conv.shape[1]
    prior = shifted(x_conv[tok_rows - (KW - 1) :], "fsdp", 1)
    leading = jnp.stack([x_conv[: KW - 1], du_scan[: KW - 1]])
    later = shifted(leading, "fsdp", -1)
    extended = jnp.concatenate([prior, x_conv, later[0]], 0)
    span = tok_rows + KW - 1
    pre_all = jnp.zeros((span, width), F32) + conv_b[None, :]
    for k in range(KW):
        pre_all = pre_all + conv_w[k][None, :] * extended[k : k + span]
    arriving = jnp.concatenate([du_scan, later[1]], 0)
    d_pre_all = arriving.astype(F32) * silu_slope(pre_all)
    d_pre = d_pre_all[:tok_rows]
    grad_x = jnp.zeros((tok_rows, width), F32)
    taps = []
    for k in range(KW):
        grad_x = grad_x + conv_w[k][None, :] * d_pre_all[KW - 1 - k : KW - 1 - k + tok_rows]
        taps.append(jnp.sum(d_pre * extended[k : k + tok_rows], 0))
    grad_w, grad_b = lax.psum((jnp.stack(taps), jnp.sum(d_pre, 0)), "fsdp")
    full_out = lax.all_gather(dout, "tp", axis=1, tiled=True)
    group_w = lax.all_gather(w_out, "fsdp", axis=0, tiled=True)
    d_gated = lax.dot_general(
        full_out, group_w, (((1,), (1,)), ((), ())), preferred_element_type=F32
    )
    gate_f = z_gate.astype(F32)
    grad_y = (d_gated * jax.nn.silu(gate_f)).astype(BF16)
    grad_z = (d_gated * y_scan.astype(F32) * silu_slope(gate_f)).astype(BF16)
    return (grad_y, grad_z, grad_x.astype(BF16), grad_w, grad_b)


def solution(mesh):
    nf, nt = mesh.shape["fsdp"], mesh.shape["tp"]

    def local(dout, w_out, *rest):
        rows = w_out.shape[0]
        kept = nf // 2 * nt * dout.size * 2
        fits = nt == 4 and nf % 2 == 0 and nf >= 6 and rows % 256 == 0 and kept <= 16 * 1024 * 1024
        body = functools.partial(fused, nf, nt) if fits else gathered
        return body(dout, w_out, *rest)

    return jax.shard_map(
        local,
        mesh=mesh,
        in_specs=(
            P("fsdp", "tp"),
            P(("tp", "fsdp"), None),
            P("fsdp", "tp"),
            P("fsdp", "tp"),
            P("fsdp", "tp"),
            P("fsdp", "tp"),
            P(None, "tp"),
            P("tp"),
        ),
        out_specs=(P("fsdp", "tp"), P("fsdp", "tp"), P("fsdp", "tp"), P(None, "tp"), P("tp")),
        check_vma=False,
    )
```

```python
import functools

import jax
import jax.numpy as jnp
from jax import lax
from jax.experimental import pallas as pl
from jax.experimental.pallas import tpu as pltpu
from jax.sharding import PartitionSpec as P

KW = 4
HALO = 16
MESH = pl.DeviceIdType.MESH
F32 = jnp.float32
BF16 = jnp.bfloat16


def silu_slope(value):
    sig = jax.nn.sigmoid(value)
    return sig * (1.0 + value * (1.0 - sig))


def kernel(
    nf, nt, dout, w, y_in, z_in, x_in, du_in, cw, cb,
    oy, oz, ox, owb,
    dbuf, wo, wn, wot, wnt, sbuf, rbuf, xb, ub, yb, zb, hp, hl, xe, ue, pe, tb, tr, tg,
    lsem, dr, zs, xs, cs, ws, wr, ss, rr, hs, hr, ts, trs, gs, gr,
):
    nz = nf // 2
    f = lax.axis_index("fsdp")
    t = lax.axis_index("tp")
    z, y = lax.div(f, 2), lax.rem(f, 2)
    x, c = lax.div(t, 2), lax.rem(t, 2)
    yf = z * 2 + 1 - y
    tx = (1 - x) * 2 + c
    tc = x * 2 + 1 - c
    tok, depth = dout.shape
    rows = w.shape[0]
    half = rows // 2
    few = tok // 2

    def remote(src, dst, send, recv, fi, ti):
        return pltpu.make_async_remote_copy(
            src_ref=src, dst_ref=dst, send_sem=send, recv_sem=recv, device_id=(fi, ti), device_id_type=MESH
        )

    loads = [
        pltpu.make_async_copy(dout.at[pl.ds(0, few)], dbuf.at[z, t, 0], lsem.at[0]),
        pltpu.make_async_copy(dout.at[pl.ds(few, few)], dbuf.at[z, t, 1], lsem.at[6]),
        pltpu.make_async_copy(x_in, xb, lsem.at[1]),
        pltpu.make_async_copy(du_in, ub, lsem.at[2]),
        pltpu.make_async_copy(w, wo, lsem.at[3]),
        pltpu.make_async_copy(y_in, yb, lsem.at[4]),
        pltpu.make_async_copy(z_in, zb, lsem.at[5]),
    ]
    for one in loads:
        one.start()

    barrier = pltpu.get_barrier_semaphore()
    for o in range(1, nf):
        pl.semaphore_signal(barrier, inc=1, device_id=(lax.rem(f + o, nf), t), device_id_type=MESH)
    pl.semaphore_signal(barrier, inc=1, device_id=(f, tx), device_id_type=MESH)
    pl.semaphore_signal(barrier, inc=1, device_id=(f, tc), device_id_type=MESH)
    pl.semaphore_wait(barrier, nf + 1)

    def halo_next():
        return remote(x_in.at[pl.ds(tok - HALO, HALO)], hp, hs.at[0], hr.at[0], f + 1, t)

    def halo_prev(i):
        src = (x_in, du_in)[i]
        return remote(src.at[pl.ds(0, HALO)], hl.at[i], hs.at[1 + i], hr.at[1 + i], f - 1, t)

    @pl.when(f < nf - 1)
    def _():
        halo_next().start()

    @pl.when(f > 0)
    def _():
        halo_prev(0).start()
        halo_prev(1).start()

    def copy_z(zz, h, sgn):
        at = dbuf.at[zz, t, h]
        return remote(at, at, zs.at[zz, h, (sgn + 1) // 2], dr.at[zz, t, h], (z + sgn) * 2 + y, t)

    def copy_x(zz, h):
        at = dbuf.at[zz, t, h]
        return remote(at, at, xs.at[zz, h], dr.at[zz, t, h], f, tx)

    def copy_c(zz, h, which):
        tt = (t, tx)[which]
        at = dbuf.at[zz, tt, h]
        return remote(at, at, cs.at[zz, h, which], dr.at[zz, tt, h], f, tc)

    def arrived(zz, tt, h):
        at = dbuf.at[zz, tt, h]
        remote(at, at, cs.at[zz, h, 0], dr.at[zz, tt, h], f, tc).wait_recv()

    def copy_w(h):
        return remote(w.at[pl.ds(h * half, half)], wn.at[h], ws.at[h], wr.at[h], yf, t)

    def valid(i):
        return (i >= 0) & (i < nz)

    def around(s, do):
        for sgn in (1, -1):
            zz = z + sgn * s

            @pl.when(valid(zz))
            def _():
                do(zz, sgn)

    for h in range(2):
        loads[h].wait()
        for sgn in (1, -1):

            @pl.when(valid(z + sgn))
            def _():
                copy_z(z, h, sgn).start()

        copy_c(z, h, 0).start()
    copy_x(z, 0).start()
    copy_w(0).start()

    @pl.when(f == 0)
    def _():
        hp[...] = jnp.zeros_like(hp)

    @pl.when(f == nf - 1)
    def _():
        hl[...] = jnp.zeros_like(hl)

    loads[2].wait()
    loads[3].wait()

    @pl.when(f > 0)
    def _():
        halo_next().wait_recv()

    @pl.when(f < nf - 1)
    def _():
        halo_prev(0).wait_recv()
        halo_prev(1).wait_recv()

    wide = tb.shape[2]

    def columns(j):
        return pl.ds(pl.multiple_of(j * wide, wide), wide)

    def conv(j, carry):
        cols = columns(j)
        xe[0:8] = hp[:, cols].astype(F32)[8:16]
        xe[8 : 8 + tok] = xb[:, cols].astype(F32)
        xe[8 + tok : 16 + tok] = hl[0, :, cols].astype(F32)[0:8]
        ue[0:tok] = ub[:, cols].astype(F32)
        ue[tok : tok + 8] = hl[1, :, cols].astype(F32)[0:8]
        taps = cw[:, cols]
        pre = cb[:, cols] + jnp.zeros((tok + 8, wide), F32)
        for k in range(KW):
            pre = pre + taps[k : k + 1] * xe[5 + k : 5 + k + tok + 8]
        pe[...] = ue[...] * silu_slope(pre)
        grad_x = jnp.zeros((tok, wide), F32)
        d_pre = pe[0:tok]
        sums = []
        for k in range(KW):
            grad_x = grad_x + taps[k : k + 1] * pe[KW - 1 - k : KW - 1 - k + tok]
            sums.append(jnp.sum(d_pre * xe[5 + k : 5 + k + tok], 0, keepdims=True))
        sums.append(jnp.sum(d_pre, 0, keepdims=True))
        ox[:, cols] = grad_x.astype(BF16)
        tb[j] = jnp.concatenate(sums + [jnp.zeros((3, wide), F32)], 0)
        return carry

    first = nf // 2
    lax.fori_loop(0, first, conv, 0)

    def tap_out(o):
        to = lax.rem(f + o, nf)
        return remote(tb.at[to], tr.at[f], ts.at[o], trs.at[f], to, t)

    def tap_in(o):
        at = lax.rem(f + o, nf)
        return remote(tb.at[at], tr.at[at], ts.at[o], trs.at[at], at, t)

    def sum_out(o):
        return remote(tg.at[f], tg.at[f], gs.at[o], gr.at[f], lax.rem(f + o, nf), t)

    def sum_in(o):
        at = lax.rem(f + o, nf)
        return remote(tg.at[at], tg.at[at], gs.at[o], gr.at[at], at, t)

    part = depth

    def result_own(zz, h):
        return remote(sbuf.at[zz, h, pl.ds(0, 2)], rbuf.at[f, h], ss.at[zz, h], rr.at[f, h], zz * 2 + y, t)

    def result_near(zz, q):
        return remote(sbuf.at[zz, :, 2 + q], rbuf.at[yf, :, q], ss.at[zz, 2 + q], rr.at[yf, q], zz * 2 + y, t)

    def dot(a, b):
        return jnp.dot(a, b, preferred_element_type=F32)

    def turn(src, dst):
        for k in range(nt):
            dst[k] = src[:, k * part : (k + 1) * part].T

    def comp_own(zz, h):
        total = jnp.zeros((few, rows), F32)
        for k in range(nt):
            total = total + dot(dbuf[zz, k, h], wot[k])
        sbuf[zz, h, 0] = total[:, :half]
        sbuf[zz, h, 1] = total[:, half:]

    def comp_near(zz, q):
        total = jnp.zeros((tok, half), F32)
        for k in range(nt):
            total = total + dot(dbuf[zz, k].reshape(tok, part), wnt[k])
        sbuf[zz, 0, 2 + q] = total[:few]
        sbuf[zz, 1, 2 + q] = total[few:]

    def forward(s, h):
        def do(zz, sgn):
            arrived(zz, t, h)

            @pl.when(valid(z - sgn))
            def _():
                copy_z(zz, h, -sgn).start()

            copy_x(zz, h).start()
            copy_c(zz, h, 0).start()

        around(s, do)

    def cross(s, h):
        def do(zz, sgn):
            arrived(zz, tx, h)
            copy_c(zz, h, 1).start()

        around(s, do) if s else do(z, 0)

    def whole(zz, h):
        arrived(zz, tc, h)
        arrived(zz, (1 - x) * 2 + 1 - c, h)

    def own_around(s, h):
        def step(i, carry):
            zz = z + (1 - 2 * i) * s

            @pl.when(valid(zz))
            def _():
                whole(zz, h)
                comp_own(zz, h)
                result_own(zz, h).start()

            return carry

        lax.fori_loop(0, 2, step, 0)

    def near_around(s, q):
        def step(i, carry):
            zz = z + (1 - 2 * i) * s

            @pl.when(valid(zz))
            def _():
                comp_near(zz, q)
                result_near(zz, q).start()

            return carry

        lax.fori_loop(0, 2, step, 0)

    def own_here(h):
        whole(z, h)
        comp_own(z, h)

    def share_taps():
        for o in range(1, nf):
            tap_out(o).start()

    def total_taps():
        total = tb[f]
        for o in range(1, nf):
            tap_in(o).wait_recv()
            total = total + tr[lax.rem(f + o, nf)]
        tg[f] = total
        for o in range(1, nf):
            sum_out(o).start()

    stages = [(s, h) for s in range(1, nz) for h in range(2)]
    last = len(stages)
    for i in range(last + 2):
        if i < last:
            forward(*stages[i])
        if i == 0:
            cross(0, 0)
        elif i <= last:
            cross(*stages[i - 1])
        if i == 1:
            copy_x(z, 1).start()
            lax.fori_loop(first, nf, conv, 0)
            share_taps()
            loads[4].wait()
            turn(wo, wot)
        if i >= 2:
            own_around(*stages[i - 2])
        if i == 2:
            copy_w(0).wait_send()
            copy_w(1).start()
        if i == 3:
            cross(0, 1)
            total_taps()
        if i == last - 1:
            copy_w(0).wait_recv()
            turn(wn.at[0], wnt)
            near_around(1, 0)
        if i == last:
            near_around(2, 0)
    own_here(0)
    own_here(1)
    for s in range(3, nz):
        near_around(s, 0)
    comp_near(z, 0)
    copy_w(1).wait_recv()
    turn(wn.at[1], wnt)
    for s in range(1, nz):
        near_around(s, 1)
    comp_near(z, 1)

    loads[5].wait()
    loads[6].wait()

    def gate(values, h, at):
        here = pl.ds(h * few, few)
        cols = pl.ds(pl.multiple_of(at, half), half)
        gate_f = zb[here, cols].astype(F32)
        sig = jax.nn.sigmoid(gate_f)
        oy[here, cols] = (values * (gate_f * sig)).astype(BF16)
        slope = sig * (1.0 + gate_f * (1.0 - sig))
        oz[here, cols] = (values * yb[here, cols].astype(F32) * slope).astype(BF16)

    for h in range(2):
        for q in range(2):
            gate(sbuf[z, h, q], h, f * rows + q * half)
            gate(sbuf[z, h, 2 + q], h, yf * rows + q * half)

    def finish(n, near):
        def step(i, carry):
            zz = z + (1 - 2 * lax.rem(i, 2)) * lax.div(i + 2, 2)

            @pl.when(valid(zz))
            def _():
                fi = zz * 2 + (1 - y if near else y)
                into = rbuf.at[fi, :, n] if near else rbuf.at[fi, n]
                remote(into, into, ss.at[zz, n], rr.at[fi, n], zz * 2 + y, t).wait_recv()
                for m in range(2):
                    h, q = (m, n) if near else (n, m)
                    gate(rbuf[fi, h, q], h, fi * rows + q * half)

            return carry

        lax.fori_loop(0, 2 * (nz - 1), step, 0)

    for near in (False, True):
        for n in range(2):
            finish(n, near)

    for o in range(1, nf):
        sum_in(o).wait_recv()
    for j in range(nf):
        owb[:, j * wide : (j + 1) * wide] = tg[j]
    for o in range(1, nf):
        tap_out(o).wait_send()
        sum_out(o).wait_send()

    @pl.when(f < nf - 1)
    def _():
        halo_next().wait_send()

    @pl.when(f > 0)
    def _():
        halo_prev(0).wait_send()
        halo_prev(1).wait_send()

    copy_w(1).wait_send()
    for h in range(2):
        for sgn in (1, -1):

            @pl.when(valid(z + sgn))
            def _():
                copy_z(z, h, sgn).wait_send()

    def sent(zz):
        for h in range(2):
            copy_x(zz, h).wait_send()
            copy_c(zz, h, 0).wait_send()
            copy_c(zz, h, 1).wait_send()

    def drain(zz, sgn):
        for h in range(2):

            @pl.when(valid(z - sgn))
            def _():
                copy_z(zz, h, -sgn).wait_send()

            result_own(zz, h).wait_send()
            result_near(zz, h).wait_send()

        sent(zz)

    sent(z)
    for s in range(1, nz):
        around(s, drain)


def fused(nf, nt, dout, w_out, y_scan, z_gate, x_conv, du_scan, conv_w, conv_b):
    tok, depth = dout.shape
    rows = w_out.shape[0]
    width = x_conv.shape[1]
    nz = nf // 2
    wide = width // nf
    anywhere = pl.BlockSpec(memory_space=pltpu.HBM)
    vmem = pl.BlockSpec(memory_space=pltpu.VMEM)
    dma = pltpu.SemaphoreType.DMA
    grad_y, grad_z, grad_x, sums = pl.pallas_call(
        functools.partial(kernel, nf, nt),
        out_shape=[jax.ShapeDtypeStruct((tok, width), BF16)] * 3 + [jax.ShapeDtypeStruct((8, width), F32)],
        in_specs=[anywhere] * 6 + [vmem] * 2,
        out_specs=[vmem] * 4,
        scratch_shapes=[
            pltpu.VMEM((nz, nt, 2, tok // 2, depth), BF16),
            pltpu.VMEM((rows, nt * depth), BF16),
            pltpu.VMEM((2, rows // 2, nt * depth), BF16),
            pltpu.VMEM((nt, depth, rows), BF16),
            pltpu.VMEM((nt, depth, rows // 2), BF16),
            pltpu.VMEM((nz, 2, 4, tok // 2, rows // 2), F32),
            pltpu.VMEM((nf, 2, 2, tok // 2, rows // 2), F32),
            pltpu.VMEM((tok, width), BF16),
            pltpu.VMEM((tok, width), BF16),
            pltpu.VMEM((tok, width), BF16),
            pltpu.VMEM((tok, width), BF16),
            pltpu.VMEM((HALO, width), BF16),
            pltpu.VMEM((2, HALO, width), BF16),
            pltpu.VMEM((tok + 16, wide), F32),
            pltpu.VMEM((tok + 8, wide), F32),
            pltpu.VMEM((tok + 8, wide), F32),
            pltpu.VMEM((nf, 8, wide), F32),
            pltpu.VMEM((nf, 8, wide), F32),
            pltpu.VMEM((nf, 8, wide), F32),
            dma((7,)),
            dma((nz, nt, 2)),
            dma((nz, 2, 2)),
            dma((nz, 2)),
            dma((nz, 2, 2)),
            dma((2,)),
            dma((2,)),
            dma((nz, 4)),
            dma((nf, 2)),
            dma((3,)),
            dma((3,)),
            dma((nf,)),
            dma((nf,)),
            dma((nf,)),
            dma((nf,)),
        ],
        compiler_params=pltpu.CompilerParams(
            collective_id=0, has_side_effects=True, vmem_limit_bytes=48 * 1024 * 1024
        ),
    )(dout, w_out, y_scan, z_gate, x_conv, du_scan, conv_w, conv_b[None, :])
    return grad_y, grad_z, grad_x, sums[:KW], sums[KW]


def shifted(block, axis, distance):
    devices = range(lax.axis_size(axis))
    route = [(i - distance, i) for i in devices if i - distance in devices]
    return lax.ppermute(block, axis, route)


def gathered(dout, w_out, y_scan, z_gate, x_conv, du_scan, conv_w, conv_b):
    tok_rows = x_conv.shape[0]
    width = x_conv.shape[1]
    prior = shifted(x_conv[tok_rows - (KW - 1) :], "fsdp", 1)
    leading = jnp.stack([x_conv[: KW - 1], du_scan[: KW - 1]])
    later = shifted(leading, "fsdp", -1)
    extended = jnp.concatenate([prior, x_conv, later[0]], 0)
    span = tok_rows + KW - 1
    pre_all = jnp.zeros((span, width), F32) + conv_b[None, :]
    for k in range(KW):
        pre_all = pre_all + conv_w[k][None, :] * extended[k : k + span]
    arriving = jnp.concatenate([du_scan, later[1]], 0)
    d_pre_all = arriving.astype(F32) * silu_slope(pre_all)
    d_pre = d_pre_all[:tok_rows]
    grad_x = jnp.zeros((tok_rows, width), F32)
    taps = []
    for k in range(KW):
        grad_x = grad_x + conv_w[k][None, :] * d_pre_all[KW - 1 - k : KW - 1 - k + tok_rows]
        taps.append(jnp.sum(d_pre * extended[k : k + tok_rows], 0))
    grad_w, grad_b = lax.psum((jnp.stack(taps), jnp.sum(d_pre, 0)), "fsdp")
    full_out = lax.all_gather(dout, "tp", axis=1, tiled=True)
    group_w = lax.all_gather(w_out, "fsdp", axis=0, tiled=True)
    d_gated = lax.dot_general(
        full_out, group_w, (((1,), (1,)), ((), ())), preferred_element_type=F32
    )
    gate_f = z_gate.astype(F32)
    grad_y = (d_gated * jax.nn.silu(gate_f)).astype(BF16)
    grad_z = (d_gated * y_scan.astype(F32) * silu_slope(gate_f)).astype(BF16)
    return (grad_y, grad_z, grad_x.astype(BF16), grad_w, grad_b)


def solution(mesh):
    nf, nt = mesh.shape["fsdp"], mesh.shape["tp"]

    def local(dout, w_out, *rest):
        rows = w_out.shape[0]
        kept = nf // 2 * nt * dout.size * 2
        fits = nt == 4 and nf % 2 == 0 and nf >= 6 and rows % 256 == 0 and kept <= 16 * 1024 * 1024
        body = functools.partial(fused, nf, nt) if fits else gathered
        return body(dout, w_out, *rest)

    return jax.shard_map(
        local,
        mesh=mesh,
        in_specs=(
            P("fsdp", "tp"),
            P(("tp", "fsdp"), None),
            P("fsdp", "tp"),
            P("fsdp", "tp"),
            P("fsdp", "tp"),
            P("fsdp", "tp"),
            P(None, "tp"),
            P("tp"),
        ),
        out_specs=(P("fsdp", "tp"), P("fsdp", "tp"), P("fsdp", "tp"), P(None, "tp"), P("tp")),
        check_vma=False,
    )
```

```python
import functools

import jax
import jax.numpy as jnp
from jax import lax
from jax.experimental import pallas as pl
from jax.experimental.pallas import tpu as pltpu
from jax.sharding import PartitionSpec as P

KW = 4
HALO = 16
MESH = pl.DeviceIdType.MESH
F32 = jnp.float32
BF16 = jnp.bfloat16


def silu_slope(value):
    sig = jax.nn.sigmoid(value)
    return sig * (1.0 + value * (1.0 - sig))


def kernel(
    nf, nt, dout, w, y_in, z_in, x_in, du_in, cw, cb,
    oy, oz, ox, ow, ob,
    dbuf, wo, wn, wot, wnt, sbuf, rbuf, xb, ub, yb, zb, hp, hl, xe, ue, pe, tb, tr, tg,
    lsem, dr, zs, xs, cs, ws, wr, ss, rr, hs, hr, ts, trs, gs, gr,
):
    nz = nf // 2
    f = lax.axis_index("fsdp")
    t = lax.axis_index("tp")
    z, y = lax.div(f, 2), lax.rem(f, 2)
    x, c = lax.div(t, 2), lax.rem(t, 2)
    yf = z * 2 + 1 - y
    tx = (1 - x) * 2 + c
    tc = x * 2 + 1 - c
    tok, depth = dout.shape
    rows = w.shape[0]
    half = rows // 2
    few = tok // 2

    def remote(src, dst, send, recv, fi, ti):
        return pltpu.make_async_remote_copy(
            src_ref=src, dst_ref=dst, send_sem=send, recv_sem=recv, device_id=(fi, ti), device_id_type=MESH
        )

    loads = [
        pltpu.make_async_copy(dout.at[pl.ds(0, few)], dbuf.at[z, t, 0], lsem.at[0]),
        pltpu.make_async_copy(dout.at[pl.ds(few, few)], dbuf.at[z, t, 1], lsem.at[6]),
        pltpu.make_async_copy(x_in, xb, lsem.at[1]),
        pltpu.make_async_copy(du_in, ub, lsem.at[2]),
        pltpu.make_async_copy(w, wo, lsem.at[3]),
        pltpu.make_async_copy(y_in, yb, lsem.at[4]),
        pltpu.make_async_copy(z_in, zb, lsem.at[5]),
    ]
    for one in loads:
        one.start()

    barrier = pltpu.get_barrier_semaphore()
    for o in range(1, nf):
        pl.semaphore_signal(barrier, inc=1, device_id=(lax.rem(f + o, nf), t), device_id_type=MESH)
    pl.semaphore_signal(barrier, inc=1, device_id=(f, tx), device_id_type=MESH)
    pl.semaphore_signal(barrier, inc=1, device_id=(f, tc), device_id_type=MESH)
    pl.semaphore_wait(barrier, nf + 1)

    def halo_next():
        return remote(x_in.at[pl.ds(tok - HALO, HALO)], hp, hs.at[0], hr.at[0], f + 1, t)

    def halo_prev(i):
        src = (x_in, du_in)[i]
        return remote(src.at[pl.ds(0, HALO)], hl.at[i], hs.at[1 + i], hr.at[1 + i], f - 1, t)

    @pl.when(f < nf - 1)
    def _():
        halo_next().start()

    @pl.when(f > 0)
    def _():
        halo_prev(0).start()
        halo_prev(1).start()

    def copy_z(zz, h, sgn):
        at = dbuf.at[zz, t, h]
        return remote(at, at, zs.at[zz, h, (sgn + 1) // 2], dr.at[zz, t, h], (z + sgn) * 2 + y, t)

    def copy_x(zz, h):
        at = dbuf.at[zz, t, h]
        return remote(at, at, xs.at[zz, h], dr.at[zz, t, h], f, tx)

    def copy_c(zz, h, which):
        tt = (t, tx)[which]
        at = dbuf.at[zz, tt, h]
        return remote(at, at, cs.at[zz, h, which], dr.at[zz, tt, h], f, tc)

    def arrived(zz, tt, h):
        at = dbuf.at[zz, tt, h]
        remote(at, at, cs.at[zz, h, 0], dr.at[zz, tt, h], f, tc).wait_recv()

    def copy_w(h):
        return remote(w.at[pl.ds(h * half, half)], wn.at[h], ws.at[h], wr.at[h], yf, t)

    def valid(i):
        return (i >= 0) & (i < nz)

    def around(s, do):
        for sgn in (1, -1):
            zz = z + sgn * s

            @pl.when(valid(zz))
            def _():
                do(zz, sgn)

    for h in range(2):
        loads[h].wait()
        for sgn in (1, -1):

            @pl.when(valid(z + sgn))
            def _():
                copy_z(z, h, sgn).start()

        copy_c(z, h, 0).start()
    copy_x(z, 0).start()
    copy_w(0).start()

    wide = tb.shape[2]

    def columns(j):
        return pl.ds(pl.multiple_of(j * wide, wide), wide)

    def conv(j, carry):
        cols = columns(j)
        xe[0:8] = hp[:, cols].astype(F32)[8:16]
        xe[8 : 8 + tok] = xb[:, cols].astype(F32)
        xe[8 + tok : 16 + tok] = hl[0, :, cols].astype(F32)[0:8]
        ue[0:tok] = ub[:, cols].astype(F32)
        ue[tok : tok + 8] = hl[1, :, cols].astype(F32)[0:8]
        taps = cw[:, cols]
        pre = cb[:, cols] + jnp.zeros((tok + 8, wide), F32)
        for k in range(KW):
            pre = pre + taps[k : k + 1] * xe[5 + k : 5 + k + tok + 8]
        pe[...] = ue[...] * silu_slope(pre)
        grad_x = jnp.zeros((tok, wide), F32)
        d_pre = pe[0:tok]
        sums = []
        for k in range(KW):
            grad_x = grad_x + taps[k : k + 1] * pe[KW - 1 - k : KW - 1 - k + tok]
            sums.append(jnp.sum(d_pre * xe[5 + k : 5 + k + tok], 0, keepdims=True))
        sums.append(jnp.sum(d_pre, 0, keepdims=True))
        ox[:, cols] = grad_x.astype(BF16)
        tb[j] = jnp.concatenate(sums + [jnp.zeros((3, wide), F32)], 0)
        return carry

    def tap_out(o):
        to = lax.rem(f + o, nf)
        return remote(tb.at[to], tr.at[f], ts.at[o], trs.at[f], to, t)

    def tap_in(o):
        at = lax.rem(f + o, nf)
        return remote(tb.at[at], tr.at[at], ts.at[o], trs.at[at], at, t)

    def sum_out(o):
        return remote(tg.at[f], tg.at[f], gs.at[o], gr.at[f], lax.rem(f + o, nf), t)

    def sum_in(o):
        at = lax.rem(f + o, nf)
        return remote(tg.at[at], tg.at[at], gs.at[o], gr.at[at], at, t)

    part = depth

    def result_own(zz, h):
        return remote(sbuf.at[zz, h, pl.ds(0, 2)], rbuf.at[f, h], ss.at[zz, h], rr.at[f, h], zz * 2 + y, t)

    def result_near(zz, q):
        return remote(sbuf.at[zz, :, 2 + q], rbuf.at[yf, :, q], ss.at[zz, 2 + q], rr.at[yf, q], zz * 2 + y, t)

    def dot(a, b):
        return jnp.dot(a, b, preferred_element_type=F32)

    def turn(src, dst):
        for k in range(nt):
            dst[k] = src[:, k * part : (k + 1) * part].T

    def comp_own(zz, h):
        total = jnp.zeros((few, rows), F32)
        for k in range(nt):
            total = total + dot(dbuf[zz, k, h], wot[k])
        sbuf[zz, h, 0] = total[:, :half]
        sbuf[zz, h, 1] = total[:, half:]

    def comp_near(zz, q):
        total = jnp.zeros((tok, half), F32)
        for k in range(nt):
            total = total + dot(dbuf[zz, k].reshape(tok, part), wnt[k])
        sbuf[zz, 0, 2 + q] = total[:few]
        sbuf[zz, 1, 2 + q] = total[few:]

    def forward(s, h):
        def do(zz, sgn):
            arrived(zz, t, h)

            @pl.when(valid(z - sgn))
            def _():
                copy_z(zz, h, -sgn).start()

            copy_x(zz, h).start()
            copy_c(zz, h, 0).start()

        around(s, do)

    def cross(s, h):
        def do(zz, sgn):
            arrived(zz, tx, h)
            copy_c(zz, h, 1).start()

        around(s, do) if s else do(z, 0)

    def whole(zz, h):
        arrived(zz, tc, h)
        arrived(zz, (1 - x) * 2 + 1 - c, h)

    def own_around(s, h):
        def step(i, carry):
            zz = z + (1 - 2 * i) * s

            @pl.when(valid(zz))
            def _():
                whole(zz, h)
                comp_own(zz, h)
                result_own(zz, h).start()

            return carry

        lax.fori_loop(0, 2, step, 0)

    def near_around(s, q):
        def step(i, carry):
            zz = z + (1 - 2 * i) * s

            @pl.when(valid(zz))
            def _():
                comp_near(zz, q)
                result_near(zz, q).start()

            return carry

        lax.fori_loop(0, 2, step, 0)

    def own_here(h):
        whole(z, h)
        comp_own(z, h)

    def share_taps():
        for o in range(1, nf):
            tap_out(o).start()

    def total_taps():
        total = tb[f]
        for o in range(1, nf):
            tap_in(o).wait_recv()
            total = total + tr[lax.rem(f + o, nf)]
        tg[f] = total
        for o in range(1, nf):
            sum_out(o).start()

    loads[4].wait()
    turn(wo, wot)

    stages = [(s, h) for s in range(1, nz) for h in range(2)]
    last = len(stages)
    for i in range(last + 2):
        if i < last:
            forward(*stages[i])
        if i == 0:
            cross(0, 0)
        elif i <= last:
            cross(*stages[i - 1])
        if i == 1:
            copy_x(z, 1).start()
        if i >= 2:
            own_around(*stages[i - 2])
        if i == 3:
            cross(0, 1)
            copy_w(0).wait_send()
            copy_w(1).start()
        if i == last - 1:
            copy_w(0).wait_recv()
            turn(wn.at[0], wnt)
            near_around(1, 0)
        if i == last:
            near_around(2, 0)
    own_here(0)
    own_here(1)
    for s in range(3, nz):
        near_around(s, 0)
    comp_near(z, 0)
    copy_w(1).wait_recv()
    turn(wn.at[1], wnt)
    for s in range(1, nz):
        near_around(s, 1)
    comp_near(z, 1)

    @pl.when(f == 0)
    def _():
        hp[...] = jnp.zeros_like(hp)

    @pl.when(f == nf - 1)
    def _():
        hl[...] = jnp.zeros_like(hl)

    loads[2].wait()
    loads[3].wait()

    @pl.when(f > 0)
    def _():
        halo_next().wait_recv()

    @pl.when(f < nf - 1)
    def _():
        halo_prev(0).wait_recv()
        halo_prev(1).wait_recv()

    lax.fori_loop(0, nf, conv, 0)
    share_taps()

    loads[5].wait()
    loads[6].wait()

    def gate(values, h, at):
        here = pl.ds(h * few, few)
        cols = pl.ds(pl.multiple_of(at, half), half)
        gate_f = zb[here, cols].astype(F32)
        sig = jax.nn.sigmoid(gate_f)
        oy[here, cols] = (values * (gate_f * sig)).astype(BF16)
        slope = sig * (1.0 + gate_f * (1.0 - sig))
        oz[here, cols] = (values * yb[here, cols].astype(F32) * slope).astype(BF16)

    for h in range(2):
        for q in range(2):
            gate(sbuf[z, h, q], h, f * rows + q * half)
            gate(sbuf[z, h, 2 + q], h, yf * rows + q * half)

    def finish(n, near):
        def step(i, carry):
            zz = z + (1 - 2 * lax.rem(i, 2)) * lax.div(i + 2, 2)

            @pl.when(valid(zz))
            def _():
                fi = zz * 2 + (1 - y if near else y)
                into = rbuf.at[fi, :, n] if near else rbuf.at[fi, n]
                remote(into, into, ss.at[zz, n], rr.at[fi, n], zz * 2 + y, t).wait_recv()
                for m in range(2):
                    h, q = (m, n) if near else (n, m)
                    gate(rbuf[fi, h, q], h, fi * rows + q * half)

            return carry

        lax.fori_loop(0, 2 * (nz - 1), step, 0)

    for n in range(2):
        finish(n, False)
    total_taps()
    for n in range(2):
        finish(n, True)

    for o in range(1, nf):
        sum_in(o).wait_recv()
    for j in range(nf):
        ow[:, j * wide : (j + 1) * wide] = tg[j, 0:KW]
        ob[:, j * wide : (j + 1) * wide] = tg[j, KW : KW + 1]
    for o in range(1, nf):
        tap_out(o).wait_send()
        sum_out(o).wait_send()

    @pl.when(f < nf - 1)
    def _():
        halo_next().wait_send()

    @pl.when(f > 0)
    def _():
        halo_prev(0).wait_send()
        halo_prev(1).wait_send()

    copy_w(1).wait_send()
    for h in range(2):
        for sgn in (1, -1):

            @pl.when(valid(z + sgn))
            def _():
                copy_z(z, h, sgn).wait_send()

    def sent(zz):
        for h in range(2):
            copy_x(zz, h).wait_send()
            copy_c(zz, h, 0).wait_send()
            copy_c(zz, h, 1).wait_send()

    def drain(zz, sgn):
        for h in range(2):

            @pl.when(valid(z - sgn))
            def _():
                copy_z(zz, h, -sgn).wait_send()

            result_own(zz, h).wait_send()
            result_near(zz, h).wait_send()

        sent(zz)

    sent(z)
    for s in range(1, nz):
        around(s, drain)


def fused(nf, nt, dout, w_out, y_scan, z_gate, x_conv, du_scan, conv_w, conv_b):
    tok, depth = dout.shape
    rows = w_out.shape[0]
    width = x_conv.shape[1]
    nz = nf // 2
    wide = width // nf
    anywhere = pl.BlockSpec(memory_space=pltpu.HBM)
    vmem = pl.BlockSpec(memory_space=pltpu.VMEM)
    dma = pltpu.SemaphoreType.DMA
    grad_y, grad_z, grad_x, grad_w, grad_b = pl.pallas_call(
        functools.partial(kernel, nf, nt),
        out_shape=[jax.ShapeDtypeStruct((tok, width), BF16)] * 3 + [jax.ShapeDtypeStruct((KW, width), F32), jax.ShapeDtypeStruct((1, width), F32)],
        in_specs=[anywhere] * 6 + [vmem] * 2,
        out_specs=[vmem] * 5,
        scratch_shapes=[
            pltpu.VMEM((nz, nt, 2, tok // 2, depth), BF16),
            pltpu.VMEM((rows, nt * depth), BF16),
            pltpu.VMEM((2, rows // 2, nt * depth), BF16),
            pltpu.VMEM((nt, depth, rows), BF16),
            pltpu.VMEM((nt, depth, rows // 2), BF16),
            pltpu.VMEM((nz, 2, 4, tok // 2, rows // 2), F32),
            pltpu.VMEM((nf, 2, 2, tok // 2, rows // 2), F32),
            pltpu.VMEM((tok, width), BF16),
            pltpu.VMEM((tok, width), BF16),
            pltpu.VMEM((tok, width), BF16),
            pltpu.VMEM((tok, width), BF16),
            pltpu.VMEM((HALO, width), BF16),
            pltpu.VMEM((2, HALO, width), BF16),
            pltpu.VMEM((tok + 16, wide), F32),
            pltpu.VMEM((tok + 8, wide), F32),
            pltpu.VMEM((tok + 8, wide), F32),
            pltpu.VMEM((nf, 8, wide), F32),
            pltpu.VMEM((nf, 8, wide), F32),
            pltpu.VMEM((nf, 8, wide), F32),
            dma((7,)),
            dma((nz, nt, 2)),
            dma((nz, 2, 2)),
            dma((nz, 2)),
            dma((nz, 2, 2)),
            dma((2,)),
            dma((2,)),
            dma((nz, 4)),
            dma((nf, 2)),
            dma((3,)),
            dma((3,)),
            dma((nf,)),
            dma((nf,)),
            dma((nf,)),
            dma((nf,)),
        ],
        compiler_params=pltpu.CompilerParams(
            collective_id=0, has_side_effects=True, vmem_limit_bytes=60 * 1024 * 1024
        ),
    )(dout, w_out, y_scan, z_gate, x_conv, du_scan, conv_w, conv_b[None, :])
    return grad_y, grad_z, grad_x, grad_w, grad_b[0]


def shifted(block, axis, distance):
    devices = range(lax.axis_size(axis))
    route = [(i - distance, i) for i in devices if i - distance in devices]
    return lax.ppermute(block, axis, route)


def gathered(dout, w_out, y_scan, z_gate, x_conv, du_scan, conv_w, conv_b):
    tok_rows = x_conv.shape[0]
    width = x_conv.shape[1]
    prior = shifted(x_conv[tok_rows - (KW - 1) :], "fsdp", 1)
    leading = jnp.stack([x_conv[: KW - 1], du_scan[: KW - 1]])
    later = shifted(leading, "fsdp", -1)
    extended = jnp.concatenate([prior, x_conv, later[0]], 0)
    span = tok_rows + KW - 1
    pre_all = jnp.zeros((span, width), F32) + conv_b[None, :]
    for k in range(KW):
        pre_all = pre_all + conv_w[k][None, :] * extended[k : k + span]
    arriving = jnp.concatenate([du_scan, later[1]], 0)
    d_pre_all = arriving.astype(F32) * silu_slope(pre_all)
    d_pre = d_pre_all[:tok_rows]
    grad_x = jnp.zeros((tok_rows, width), F32)
    taps = []
    for k in range(KW):
        grad_x = grad_x + conv_w[k][None, :] * d_pre_all[KW - 1 - k : KW - 1 - k + tok_rows]
        taps.append(jnp.sum(d_pre * extended[k : k + tok_rows], 0))
    grad_w, grad_b = lax.psum((jnp.stack(taps), jnp.sum(d_pre, 0)), "fsdp")
    full_out = lax.all_gather(dout, "tp", axis=1, tiled=True)
    group_w = lax.all_gather(w_out, "fsdp", axis=0, tiled=True)
    d_gated = lax.dot_general(
        full_out, group_w, (((1,), (1,)), ((), ())), preferred_element_type=F32
    )
    gate_f = z_gate.astype(F32)
    grad_y = (d_gated * jax.nn.silu(gate_f)).astype(BF16)
    grad_z = (d_gated * y_scan.astype(F32) * silu_slope(gate_f)).astype(BF16)
    return (grad_y, grad_z, grad_x.astype(BF16), grad_w, grad_b)


def solution(mesh):
    nf, nt = mesh.shape["fsdp"], mesh.shape["tp"]

    def local(dout, w_out, *rest):
        rows = w_out.shape[0]
        kept = nf // 2 * nt * dout.size * 2
        fits = nt == 4 and nf % 2 == 0 and nf >= 6 and rows % 256 == 0 and kept <= 16 * 1024 * 1024
        body = functools.partial(fused, nf, nt) if fits else gathered
        return body(dout, w_out, *rest)

    return jax.shard_map(
        local,
        mesh=mesh,
        in_specs=(
            P("fsdp", "tp"),
            P(("tp", "fsdp"), None),
            P("fsdp", "tp"),
            P("fsdp", "tp"),
            P("fsdp", "tp"),
            P("fsdp", "tp"),
            P(None, "tp"),
            P("tp"),
        ),
        out_specs=(P("fsdp", "tp"), P("fsdp", "tp"), P("fsdp", "tp"), P(None, "tp"), P("tp")),
        check_vma=False,
    )
```

```python
import functools

import jax
import jax.numpy as jnp
from jax import lax
from jax.experimental import pallas as pl
from jax.experimental.pallas import tpu as pltpu
from jax.sharding import PartitionSpec as P

KW = 4
HALO = 16
MESH = pl.DeviceIdType.MESH
F32 = jnp.float32
BF16 = jnp.bfloat16


def silu_slope(value):
    sig = jax.nn.sigmoid(value)
    return sig * (1.0 + value * (1.0 - sig))


def kernel(
    nf, nt, dout, w, y_in, z_in, x_in, du_in, cw, cb,
    oy, oz, ox, ow, ob,
    dbuf, wo, wn, wot, wnt, sbuf, rbuf, xb, ub, yb, zb, hp, hl, xe, ue, pe, tb, tr, tg,
    lsem, dr, zs, xs, cs, ws, wr, ss, rr, hs, hr, ts, trs, gs, gr,
):
    nz = nf // 2
    f = lax.axis_index("fsdp")
    t = lax.axis_index("tp")
    z, y = lax.div(f, 2), lax.rem(f, 2)
    x, c = lax.div(t, 2), lax.rem(t, 2)
    yf = z * 2 + 1 - y
    tx = (1 - x) * 2 + c
    tc = x * 2 + 1 - c
    tok, depth = dout.shape
    rows = w.shape[0]
    half = rows // 2
    few = tok // 2

    def remote(src, dst, send, recv, fi, ti):
        return pltpu.make_async_remote_copy(
            src_ref=src, dst_ref=dst, send_sem=send, recv_sem=recv, device_id=(fi, ti), device_id_type=MESH
        )

    loads = [
        pltpu.make_async_copy(dout.at[pl.ds(0, few)], dbuf.at[z, t, 0], lsem.at[0]),
        pltpu.make_async_copy(dout.at[pl.ds(few, few)], dbuf.at[z, t, 1], lsem.at[6]),
        pltpu.make_async_copy(x_in, xb, lsem.at[1]),
        pltpu.make_async_copy(du_in, ub, lsem.at[2]),
        pltpu.make_async_copy(w, wo, lsem.at[3]),
        pltpu.make_async_copy(y_in, yb, lsem.at[4]),
        pltpu.make_async_copy(z_in, zb, lsem.at[5]),
    ]
    for one in loads:
        one.start()

    barrier = pltpu.get_barrier_semaphore()
    for o in range(1, nf):
        pl.semaphore_signal(barrier, inc=1, device_id=(lax.rem(f + o, nf), t), device_id_type=MESH)
    pl.semaphore_signal(barrier, inc=1, device_id=(f, tx), device_id_type=MESH)
    pl.semaphore_signal(barrier, inc=1, device_id=(f, tc), device_id_type=MESH)
    pl.semaphore_wait(barrier, nf + 1)

    def halo_next():
        return remote(x_in.at[pl.ds(tok - HALO, HALO)], hp, hs.at[0], hr.at[0], f + 1, t)

    def halo_prev(i):
        src = (x_in, du_in)[i]
        return remote(src.at[pl.ds(0, HALO)], hl.at[i], hs.at[1 + i], hr.at[1 + i], f - 1, t)

    @pl.when(f < nf - 1)
    def _():
        halo_next().start()

    @pl.when(f > 0)
    def _():
        halo_prev(0).start()
        halo_prev(1).start()

    def copy_z(zz, h, sgn):
        at = dbuf.at[zz, t, h]
        return remote(at, at, zs.at[zz, h, (sgn + 1) // 2], dr.at[zz, t, h], (z + sgn) * 2 + y, t)

    def copy_x(zz, h):
        at = dbuf.at[zz, t, h]
        return remote(at, at, xs.at[zz, h], dr.at[zz, t, h], f, tx)

    def copy_c(zz, h, which):
        tt = (t, tx)[which]
        at = dbuf.at[zz, tt, h]
        return remote(at, at, cs.at[zz, h, which], dr.at[zz, tt, h], f, tc)

    def arrived(zz, tt, h):
        at = dbuf.at[zz, tt, h]
        remote(at, at, cs.at[zz, h, 0], dr.at[zz, tt, h], f, tc).wait_recv()

    def copy_w(h):
        return remote(w.at[pl.ds(h * half, half)], wn.at[h], ws.at[h], wr.at[h], yf, t)

    def valid(i):
        return (i >= 0) & (i < nz)

    def around(s, do):
        for sgn in (1, -1):
            zz = z + sgn * s

            @pl.when(valid(zz))
            def _():
                do(zz, sgn)

    for h in range(2):
        loads[h].wait()
        for sgn in (1, -1):

            @pl.when(valid(z + sgn))
            def _():
                copy_z(z, h, sgn).start()

        copy_c(z, h, 0).start()
    copy_x(z, 0).start()
    for h in range(2):
        copy_w(h).start()

    wide = tb.shape[2]

    def columns(j):
        return pl.ds(pl.multiple_of(j * wide, wide), wide)

    def conv(j, carry):
        cols = columns(j)
        xe[0:8] = hp[:, cols].astype(F32)[8:16]
        xe[8 : 8 + tok] = xb[:, cols].astype(F32)
        xe[8 + tok : 16 + tok] = hl[0, :, cols].astype(F32)[0:8]
        ue[0:tok] = ub[:, cols].astype(F32)
        ue[tok : tok + 8] = hl[1, :, cols].astype(F32)[0:8]
        taps = cw[:, cols]
        pre = cb[:, cols] + jnp.zeros((tok + 8, wide), F32)
        for k in range(KW):
            pre = pre + taps[k : k + 1] * xe[5 + k : 5 + k + tok + 8]
        pe[...] = ue[...] * silu_slope(pre)
        grad_x = jnp.zeros((tok, wide), F32)
        d_pre = pe[0:tok]
        sums = []
        for k in range(KW):
            grad_x = grad_x + taps[k : k + 1] * pe[KW - 1 - k : KW - 1 - k + tok]
            sums.append(jnp.sum(d_pre * xe[5 + k : 5 + k + tok], 0, keepdims=True))
        sums.append(jnp.sum(d_pre, 0, keepdims=True))
        ox[:, cols] = grad_x.astype(BF16)
        tb[j] = jnp.concatenate(sums + [jnp.zeros((3, wide), F32)], 0)
        return carry

    def tap_out(o):
        to = lax.rem(f + o, nf)
        return remote(tb.at[to], tr.at[f], ts.at[o], trs.at[f], to, t)

    def tap_in(o):
        at = lax.rem(f + o, nf)
        return remote(tb.at[at], tr.at[at], ts.at[o], trs.at[at], at, t)

    def sum_out(o):
        return remote(tg.at[f], tg.at[f], gs.at[o], gr.at[f], lax.rem(f + o, nf), t)

    def sum_in(o):
        at = lax.rem(f + o, nf)
        return remote(tg.at[at], tg.at[at], gs.at[o], gr.at[at], at, t)

    part = depth

    def result_own(zz, h):
        return remote(sbuf.at[zz, h, pl.ds(0, 2)], rbuf.at[f, h], ss.at[zz, h], rr.at[f, h], zz * 2 + y, t)

    def result_near(zz, q):
        return remote(sbuf.at[zz, :, 2 + q], rbuf.at[yf, :, q], ss.at[zz, 2 + q], rr.at[yf, q], zz * 2 + y, t)

    def dot(a, b):
        return jnp.dot(a, b, preferred_element_type=F32)

    def turn(src, dst):
        for k in range(nt):
            dst[k] = src[:, k * part : (k + 1) * part].T

    def comp_own(zz, h):
        total = jnp.zeros((few, rows), F32)
        for k in range(nt):
            total = total + dot(dbuf[zz, k, h], wot[k])
        sbuf[zz, h, 0] = total[:, :half]
        sbuf[zz, h, 1] = total[:, half:]

    def comp_near(zz, q):
        total = jnp.zeros((tok, half), F32)
        for k in range(nt):
            total = total + dot(dbuf[zz, k].reshape(tok, part), wnt[k])
        sbuf[zz, 0, 2 + q] = total[:few]
        sbuf[zz, 1, 2 + q] = total[few:]

    def forward(s, h):
        def do(zz, sgn):
            arrived(zz, t, h)

            @pl.when(valid(z - sgn))
            def _():
                copy_z(zz, h, -sgn).start()

            copy_x(zz, h).start()
            copy_c(zz, h, 0).start()

        around(s, do)

    def cross(s, h):
        def do(zz, sgn):
            arrived(zz, tx, h)
            copy_c(zz, h, 1).start()

        around(s, do) if s else do(z, 0)

    def whole(zz, h):
        arrived(zz, tc, h)
        arrived(zz, (1 - x) * 2 + 1 - c, h)

    def own_around(s, h):
        def step(i, carry):
            zz = z + (1 - 2 * i) * s

            @pl.when(valid(zz))
            def _():
                whole(zz, h)
                comp_own(zz, h)
                result_own(zz, h).start()

            return carry

        lax.fori_loop(0, 2, step, 0)

    def near_around(s, q):
        def step(i, carry):
            zz = z + (1 - 2 * i) * s

            @pl.when(valid(zz))
            def _():
                comp_near(zz, q)
                result_near(zz, q).start()

            return carry

        lax.fori_loop(0, 2, step, 0)

    def own_here(h):
        whole(z, h)
        comp_own(z, h)

    def share_taps():
        for o in range(1, nf):
            tap_out(o).start()

    def total_taps():
        total = tb[f]
        for o in range(1, nf):
            tap_in(o).wait_recv()
            total = total + tr[lax.rem(f + o, nf)]
        tg[f] = total
        for o in range(1, nf):
            sum_out(o).start()

    loads[4].wait()
    turn(wo, wot)

    @pl.when(f == 0)
    def _():
        hp[...] = jnp.zeros_like(hp)

    @pl.when(f == nf - 1)
    def _():
        hl[...] = jnp.zeros_like(hl)

    loads[2].wait()
    loads[3].wait()

    @pl.when(f > 0)
    def _():
        halo_next().wait_recv()

    @pl.when(f < nf - 1)
    def _():
        halo_prev(0).wait_recv()
        halo_prev(1).wait_recv()

    stages = [(s, h) for s in range(1, nz) for h in range(2)]
    last = len(stages)
    for i in range(last + 2):
        if i < last:
            forward(*stages[i])
        if i == 0:
            cross(0, 0)
        elif i <= last:
            cross(*stages[i - 1])
        if i == 1:
            copy_x(z, 1).start()
        conv(i, 0)
        if i >= 2:
            own_around(*stages[i - 2])
        if i == 3:
            cross(0, 1)
        if i == last - 1:
            copy_w(0).wait_recv()
            turn(wn.at[0], wnt)
            near_around(1, 0)
        if i == last:
            near_around(2, 0)
    lax.fori_loop(last + 2, nf, conv, 0)
    share_taps()
    own_here(0)
    own_here(1)
    for s in range(3, nz):
        near_around(s, 0)
    comp_near(z, 0)
    copy_w(1).wait_recv()
    turn(wn.at[1], wnt)
    for s in range(1, nz):
        near_around(s, 1)
    comp_near(z, 1)
    total_taps()

    loads[5].wait()
    loads[6].wait()

    def gate(values, h, at):
        here = pl.ds(h * few, few)
        cols = pl.ds(pl.multiple_of(at, half), half)
        gate_f = zb[here, cols].astype(F32)
        sig = jax.nn.sigmoid(gate_f)
        oy[here, cols] = (values * (gate_f * sig)).astype(BF16)
        slope = sig * (1.0 + gate_f * (1.0 - sig))
        oz[here, cols] = (values * yb[here, cols].astype(F32) * slope).astype(BF16)

    for h in range(2):
        for q in range(2):
            gate(sbuf[z, h, q], h, f * rows + q * half)
            gate(sbuf[z, h, 2 + q], h, yf * rows + q * half)

    def finish(n, near):
        def step(i, carry):
            zz = z + (1 - 2 * lax.rem(i, 2)) * lax.div(i + 2, 2)

            @pl.when(valid(zz))
            def _():
                fi = zz * 2 + (1 - y if near else y)
                into = rbuf.at[fi, :, n] if near else rbuf.at[fi, n]
                remote(into, into, ss.at[zz, n], rr.at[fi, n], zz * 2 + y, t).wait_recv()
                for m in range(2):
                    h, q = (m, n) if near else (n, m)
                    gate(rbuf[fi, h, q], h, fi * rows + q * half)

            return carry

        lax.fori_loop(0, 2 * (nz - 1), step, 0)

    for n in range(2):
        finish(n, False)
    for n in range(2):
        finish(n, True)

    for o in range(1, nf):
        sum_in(o).wait_recv()
    for j in range(nf):
        ow[:, j * wide : (j + 1) * wide] = tg[j, 0:KW]
        ob[:, j * wide : (j + 1) * wide] = tg[j, KW : KW + 1]
    for o in range(1, nf):
        tap_out(o).wait_send()
        sum_out(o).wait_send()

    @pl.when(f < nf - 1)
    def _():
        halo_next().wait_send()

    @pl.when(f > 0)
    def _():
        halo_prev(0).wait_send()
        halo_prev(1).wait_send()

    for h in range(2):
        copy_w(h).wait_send()
    for h in range(2):
        for sgn in (1, -1):

            @pl.when(valid(z + sgn))
            def _():
                copy_z(z, h, sgn).wait_send()

    def sent(zz):
        for h in range(2):
            copy_x(zz, h).wait_send()
            copy_c(zz, h, 0).wait_send()
            copy_c(zz, h, 1).wait_send()

    def drain(zz, sgn):
        for h in range(2):

            @pl.when(valid(z - sgn))
            def _():
                copy_z(zz, h, -sgn).wait_send()

            result_own(zz, h).wait_send()
            result_near(zz, h).wait_send()

        sent(zz)

    sent(z)
    for s in range(1, nz):
        around(s, drain)


def fused(nf, nt, dout, w_out, y_scan, z_gate, x_conv, du_scan, conv_w, conv_b):
    tok, depth = dout.shape
    rows = w_out.shape[0]
    width = x_conv.shape[1]
    nz = nf // 2
    wide = width // nf
    anywhere = pl.BlockSpec(memory_space=pltpu.HBM)
    vmem = pl.BlockSpec(memory_space=pltpu.VMEM)
    dma = pltpu.SemaphoreType.DMA
    grad_y, grad_z, grad_x, grad_w, grad_b = pl.pallas_call(
        functools.partial(kernel, nf, nt),
        out_shape=[jax.ShapeDtypeStruct((tok, width), BF16)] * 3 + [jax.ShapeDtypeStruct((KW, width), F32), jax.ShapeDtypeStruct((1, width), F32)],
        in_specs=[anywhere] * 6 + [vmem] * 2,
        out_specs=[vmem] * 5,
        scratch_shapes=[
            pltpu.VMEM((nz, nt, 2, tok // 2, depth), BF16),
            pltpu.VMEM((rows, nt * depth), BF16),
            pltpu.VMEM((2, rows // 2, nt * depth), BF16),
            pltpu.VMEM((nt, depth, rows), BF16),
            pltpu.VMEM((nt, depth, rows // 2), BF16),
            pltpu.VMEM((nz, 2, 4, tok // 2, rows // 2), F32),
            pltpu.VMEM((nf, 2, 2, tok // 2, rows // 2), F32),
            pltpu.VMEM((tok, width), BF16),
            pltpu.VMEM((tok, width), BF16),
            pltpu.VMEM((tok, width), BF16),
            pltpu.VMEM((tok, width), BF16),
            pltpu.VMEM((HALO, width), BF16),
            pltpu.VMEM((2, HALO, width), BF16),
            pltpu.VMEM((tok + 16, wide), F32),
            pltpu.VMEM((tok + 8, wide), F32),
            pltpu.VMEM((tok + 8, wide), F32),
            pltpu.VMEM((nf, 8, wide), F32),
            pltpu.VMEM((nf, 8, wide), F32),
            pltpu.VMEM((nf, 8, wide), F32),
            dma((7,)),
            dma((nz, nt, 2)),
            dma((nz, 2, 2)),
            dma((nz, 2)),
            dma((nz, 2, 2)),
            dma((2,)),
            dma((2,)),
            dma((nz, 4)),
            dma((nf, 2)),
            dma((3,)),
            dma((3,)),
            dma((nf,)),
            dma((nf,)),
            dma((nf,)),
            dma((nf,)),
        ],
        compiler_params=pltpu.CompilerParams(
            collective_id=0, has_side_effects=True, vmem_limit_bytes=48 * 1024 * 1024
        ),
    )(dout, w_out, y_scan, z_gate, x_conv, du_scan, conv_w, conv_b[None, :])
    return grad_y, grad_z, grad_x, grad_w, grad_b[0]


def shifted(block, axis, distance):
    devices = range(lax.axis_size(axis))
    route = [(i - distance, i) for i in devices if i - distance in devices]
    return lax.ppermute(block, axis, route)


def gathered(dout, w_out, y_scan, z_gate, x_conv, du_scan, conv_w, conv_b):
    tok_rows = x_conv.shape[0]
    width = x_conv.shape[1]
    prior = shifted(x_conv[tok_rows - (KW - 1) :], "fsdp", 1)
    leading = jnp.stack([x_conv[: KW - 1], du_scan[: KW - 1]])
    later = shifted(leading, "fsdp", -1)
    extended = jnp.concatenate([prior, x_conv, later[0]], 0)
    span = tok_rows + KW - 1
    pre_all = jnp.zeros((span, width), F32) + conv_b[None, :]
    for k in range(KW):
        pre_all = pre_all + conv_w[k][None, :] * extended[k : k + span]
    arriving = jnp.concatenate([du_scan, later[1]], 0)
    d_pre_all = arriving.astype(F32) * silu_slope(pre_all)
    d_pre = d_pre_all[:tok_rows]
    grad_x = jnp.zeros((tok_rows, width), F32)
    taps = []
    for k in range(KW):
        grad_x = grad_x + conv_w[k][None, :] * d_pre_all[KW - 1 - k : KW - 1 - k + tok_rows]
        taps.append(jnp.sum(d_pre * extended[k : k + tok_rows], 0))
    grad_w, grad_b = lax.psum((jnp.stack(taps), jnp.sum(d_pre, 0)), "fsdp")
    full_out = lax.all_gather(dout, "tp", axis=1, tiled=True)
    group_w = lax.all_gather(w_out, "fsdp", axis=0, tiled=True)
    d_gated = lax.dot_general(
        full_out, group_w, (((1,), (1,)), ((), ())), preferred_element_type=F32
    )
    gate_f = z_gate.astype(F32)
    grad_y = (d_gated * jax.nn.silu(gate_f)).astype(BF16)
    grad_z = (d_gated * y_scan.astype(F32) * silu_slope(gate_f)).astype(BF16)
    return (grad_y, grad_z, grad_x.astype(BF16), grad_w, grad_b)


def solution(mesh):
    nf, nt = mesh.shape["fsdp"], mesh.shape["tp"]

    def local(dout, w_out, *rest):
        rows = w_out.shape[0]
        kept = nf // 2 * nt * dout.size * 2
        fits = nt == 4 and nf % 2 == 0 and nf >= 8 and rows % 256 == 0 and kept <= 16 * 1024 * 1024
        body = functools.partial(fused, nf, nt) if fits else gathered
        return body(dout, w_out, *rest)

    return jax.shard_map(
        local,
        mesh=mesh,
        in_specs=(
            P("fsdp", "tp"),
            P(("tp", "fsdp"), None),
            P("fsdp", "tp"),
            P("fsdp", "tp"),
            P("fsdp", "tp"),
            P("fsdp", "tp"),
            P(None, "tp"),
            P("tp"),
        ),
        out_specs=(P("fsdp", "tp"), P("fsdp", "tp"), P("fsdp", "tp"), P(None, "tp"), P("tp")),
        check_vma=False,
    )
```

```python
import functools

import jax
import jax.numpy as jnp
from jax import lax
from jax.experimental import pallas as pl
from jax.experimental.pallas import tpu as pltpu
from jax.sharding import PartitionSpec as P

KW = 4
HALO = 16
MESH = pl.DeviceIdType.MESH
F32 = jnp.float32
BF16 = jnp.bfloat16


def silu_slope(value):
    sig = jax.nn.sigmoid(value)
    return sig * (1.0 + value * (1.0 - sig))


def kernel(
    nf, nt, dout, w, y_in, z_in, x_in, du_in, cw, cb,
    oy, oz, ox, ow, ob,
    dbuf, wo, wn, wot, wnt, sbuf, rbuf, xb, ub, yb, zb, hp, hl, xe, ue, pe, tb, tr, tg,
    lsem, dr, zs, xs, cs, ws, wr, ss, rr, hs, hr, ts, trs, gs, gr,
):
    nz = nf // 2
    f = lax.axis_index("fsdp")
    t = lax.axis_index("tp")
    z, y = lax.div(f, 2), lax.rem(f, 2)
    x, c = lax.div(t, 2), lax.rem(t, 2)
    yf = z * 2 + 1 - y
    tx = (1 - x) * 2 + c
    tc = x * 2 + 1 - c
    tok, depth = dout.shape
    rows = w.shape[0]
    half = rows // 2
    few = tok // 2

    def remote(src, dst, send, recv, fi, ti):
        return pltpu.make_async_remote_copy(
            src_ref=src, dst_ref=dst, send_sem=send, recv_sem=recv, device_id=(fi, ti), device_id_type=MESH
        )

    loads = [
        pltpu.make_async_copy(dout.at[pl.ds(0, few)], dbuf.at[z, t, 0], lsem.at[0]),
        pltpu.make_async_copy(dout.at[pl.ds(few, few)], dbuf.at[z, t, 1], lsem.at[6]),
        pltpu.make_async_copy(x_in, xb, lsem.at[1]),
        pltpu.make_async_copy(du_in, ub, lsem.at[2]),
        pltpu.make_async_copy(w, wo, lsem.at[3]),
        pltpu.make_async_copy(y_in, yb, lsem.at[4]),
        pltpu.make_async_copy(z_in, zb, lsem.at[5]),
    ]
    for one in loads:
        one.start()

    barrier = pltpu.get_barrier_semaphore()
    for o in range(1, nf):
        pl.semaphore_signal(barrier, inc=1, device_id=(lax.rem(f + o, nf), t), device_id_type=MESH)
    pl.semaphore_signal(barrier, inc=1, device_id=(f, tx), device_id_type=MESH)
    pl.semaphore_signal(barrier, inc=1, device_id=(f, tc), device_id_type=MESH)
    pl.semaphore_wait(barrier, nf + 1)

    def halo_next():
        return remote(x_in.at[pl.ds(tok - HALO, HALO)], hp, hs.at[0], hr.at[0], f + 1, t)

    def halo_prev(i):
        src = (x_in, du_in)[i]
        return remote(src.at[pl.ds(0, HALO)], hl.at[i], hs.at[1 + i], hr.at[1 + i], f - 1, t)

    @pl.when(f < nf - 1)
    def _():
        halo_next().start()

    @pl.when(f > 0)
    def _():
        halo_prev(0).start()
        halo_prev(1).start()

    def copy_z(zz, h, sgn):
        at = dbuf.at[zz, t, h]
        return remote(at, at, zs.at[zz, h, (sgn + 1) // 2], dr.at[zz, t, h], (z + sgn) * 2 + y, t)

    def copy_x(zz, h):
        at = dbuf.at[zz, t, h]
        return remote(at, at, xs.at[zz, h], dr.at[zz, t, h], f, tx)

    def copy_c(zz, h, which):
        tt = (t, tx)[which]
        at = dbuf.at[zz, tt, h]
        return remote(at, at, cs.at[zz, h, which], dr.at[zz, tt, h], f, tc)

    def arrived(zz, tt, h):
        at = dbuf.at[zz, tt, h]
        remote(at, at, cs.at[zz, h, 0], dr.at[zz, tt, h], f, tc).wait_recv()

    def copy_w(i):
        src = w.at[pl.ds(i * (half // 2), half // 2)]
        return remote(src, wn.at[i // 2, pl.ds(i % 2 * (half // 2), half // 2)], ws.at[i], wr.at[i], yf, t)

    def valid(i):
        return (i >= 0) & (i < nz)

    def around(s, do):
        for sgn in (1, -1):
            zz = z + sgn * s

            @pl.when(valid(zz))
            def _():
                do(zz, sgn)

    for h in range(2):
        loads[h].wait()
        for sgn in (1, -1):

            @pl.when(valid(z + sgn))
            def _():
                copy_z(z, h, sgn).start()

        copy_c(z, h, 0).start()
    copy_x(z, 0).start()
    copy_w(0).start()

    wide = tb.shape[2]

    def columns(j):
        return pl.ds(pl.multiple_of(j * wide, wide), wide)

    def conv(j, carry):
        cols = columns(j)
        xe[0:8] = hp[:, cols].astype(F32)[8:16]
        xe[8 : 8 + tok] = xb[:, cols].astype(F32)
        xe[8 + tok : 16 + tok] = hl[0, :, cols].astype(F32)[0:8]
        ue[0:tok] = ub[:, cols].astype(F32)
        ue[tok : tok + 8] = hl[1, :, cols].astype(F32)[0:8]
        taps = cw[:, cols]
        pre = cb[:, cols] + jnp.zeros((tok + 8, wide), F32)
        for k in range(KW):
            pre = pre + taps[k : k + 1] * xe[5 + k : 5 + k + tok + 8]
        pe[...] = ue[...] * silu_slope(pre)
        grad_x = jnp.zeros((tok, wide), F32)
        d_pre = pe[0:tok]
        sums = []
        for k in range(KW):
            grad_x = grad_x + taps[k : k + 1] * pe[KW - 1 - k : KW - 1 - k + tok]
            sums.append(jnp.sum(d_pre * xe[5 + k : 5 + k + tok], 0, keepdims=True))
        sums.append(jnp.sum(d_pre, 0, keepdims=True))
        ox[:, cols] = grad_x.astype(BF16)
        tb[j] = jnp.concatenate(sums + [jnp.zeros((3, wide), F32)], 0)
        return carry

    def tap_out(o):
        to = lax.rem(f + o, nf)
        return remote(tb.at[to], tr.at[f], ts.at[o], trs.at[f], to, t)

    def tap_in(o):
        at = lax.rem(f + o, nf)
        return remote(tb.at[at], tr.at[at], ts.at[o], trs.at[at], at, t)

    def sum_out(o):
        return remote(tg.at[f], tg.at[f], gs.at[o], gr.at[f], lax.rem(f + o, nf), t)

    def sum_in(o):
        at = lax.rem(f + o, nf)
        return remote(tg.at[at], tg.at[at], gs.at[o], gr.at[at], at, t)

    part = depth

    def result_own(zz, h):
        return remote(sbuf.at[zz, h, pl.ds(0, 2)], rbuf.at[f, h], ss.at[zz, h], rr.at[f, h], zz * 2 + y, t)

    def result_near(zz, q):
        return remote(sbuf.at[zz, :, 2 + q], rbuf.at[yf, :, q], ss.at[zz, 2 + q], rr.at[yf, q], zz * 2 + y, t)

    def dot(a, b):
        return jnp.dot(a, b, preferred_element_type=F32)

    def turn(src, dst):
        for k in range(nt):
            dst[k] = src[:, k * part : (k + 1) * part].T

    def comp_own(zz, h):
        total = jnp.zeros((few, rows), F32)
        for k in range(nt):
            total = total + dot(dbuf[zz, k, h], wot[k])
        sbuf[zz, h, 0] = total[:, :half]
        sbuf[zz, h, 1] = total[:, half:]

    def comp_near(zz, q):
        total = jnp.zeros((tok, half), F32)
        for k in range(nt):
            total = total + dot(dbuf[zz, k].reshape(tok, part), wnt[k])
        sbuf[zz, 0, 2 + q] = total[:few]
        sbuf[zz, 1, 2 + q] = total[few:]

    def forward(s, h):
        def do(zz, sgn):
            arrived(zz, t, h)

            @pl.when(valid(z - sgn))
            def _():
                copy_z(zz, h, -sgn).start()

            copy_x(zz, h).start()
            copy_c(zz, h, 0).start()

        around(s, do)

    def cross(s, h):
        def do(zz, sgn):
            arrived(zz, tx, h)
            copy_c(zz, h, 1).start()

        around(s, do) if s else do(z, 0)

    def whole(zz, h):
        arrived(zz, tc, h)
        arrived(zz, (1 - x) * 2 + 1 - c, h)

    def own_around(s, h):
        def step(i, carry):
            zz = z + (1 - 2 * i) * s

            @pl.when(valid(zz))
            def _():
                whole(zz, h)
                comp_own(zz, h)
                result_own(zz, h).start()

            return carry

        lax.fori_loop(0, 2, step, 0)

    def near_around(s, q):
        def step(i, carry):
            zz = z + (1 - 2 * i) * s

            @pl.when(valid(zz))
            def _():
                comp_near(zz, q)
                result_near(zz, q).start()

            return carry

        lax.fori_loop(0, 2, step, 0)

    def own_here(h):
        whole(z, h)
        comp_own(z, h)

    def share_taps():
        for o in range(1, nf):
            tap_out(o).start()

    def total_taps():
        total = tb[f]
        for o in range(1, nf):
            tap_in(o).wait_recv()
            total = total + tr[lax.rem(f + o, nf)]
        tg[f] = total
        for o in range(1, nf):
            sum_out(o).start()

    loads[4].wait()
    turn(wo, wot)

    @pl.when(f == 0)
    def _():
        hp[...] = jnp.zeros_like(hp)

    @pl.when(f == nf - 1)
    def _():
        hl[...] = jnp.zeros_like(hl)

    loads[2].wait()
    loads[3].wait()

    @pl.when(f > 0)
    def _():
        halo_next().wait_recv()

    @pl.when(f < nf - 1)
    def _():
        halo_prev(0).wait_recv()
        halo_prev(1).wait_recv()

    stages = [(s, h) for s in range(1, nz) for h in range(2)]
    last = len(stages)
    for i in range(last + 2):
        if i < last:
            forward(*stages[i])
        if i == 0:
            cross(0, 0)
        elif i <= last:
            cross(*stages[i - 1])
        if i == 1:
            copy_x(z, 1).start()
        if i < 3:
            copy_w(i + 1).start()
        conv(i, 0)
        if i >= 2:
            own_around(*stages[i - 2])
        if i == 3:
            cross(0, 1)
        if i == last - 1:
            copy_w(0).wait_recv()
            copy_w(1).wait_recv()
            turn(wn.at[0], wnt)
            near_around(1, 0)
        if i == last:
            near_around(2, 0)
    lax.fori_loop(last + 2, nf, conv, 0)
    share_taps()
    own_here(0)
    own_here(1)
    for s in range(3, nz):
        near_around(s, 0)
    comp_near(z, 0)
    loads[5].wait()
    loads[6].wait()

    def gate(values, h, at):
        here = pl.ds(h * few, few)
        cols = pl.ds(pl.multiple_of(at, half), half)
        gate_f = zb[here, cols].astype(F32)
        sig = jax.nn.sigmoid(gate_f)
        oy[here, cols] = (values * (gate_f * sig)).astype(BF16)
        slope = sig * (1.0 + gate_f * (1.0 - sig))
        oz[here, cols] = (values * yb[here, cols].astype(F32) * slope).astype(BF16)

    for h in range(2):
        for q in range(2):
            gate(sbuf[z, h, q], h, f * rows + q * half)
    copy_w(2).wait_recv()
    copy_w(3).wait_recv()
    turn(wn.at[1], wnt)
    for s in range(1, nz):
        near_around(s, 1)
    comp_near(z, 1)
    total_taps()

    for h in range(2):
        for q in range(2):
            gate(sbuf[z, h, 2 + q], h, yf * rows + q * half)

    def finish(n, near):
        def step(i, carry):
            zz = z + (1 - 2 * lax.rem(i, 2)) * lax.div(i + 2, 2)

            @pl.when(valid(zz))
            def _():
                fi = zz * 2 + (1 - y if near else y)
                into = rbuf.at[fi, :, n] if near else rbuf.at[fi, n]
                remote(into, into, ss.at[zz, n], rr.at[fi, n], zz * 2 + y, t).wait_recv()
                for m in range(2):
                    h, q = (m, n) if near else (n, m)
                    gate(rbuf[fi, h, q], h, fi * rows + q * half)

            return carry

        lax.fori_loop(0, 2 * (nz - 1), step, 0)

    for n in range(2):
        finish(n, False)
    for n in range(2):
        finish(n, True)

    for o in range(1, nf):
        sum_in(o).wait_recv()
    for j in range(nf):
        ow[:, j * wide : (j + 1) * wide] = tg[j, 0:KW]
        ob[:, j * wide : (j + 1) * wide] = tg[j, KW : KW + 1]
    for o in range(1, nf):
        tap_out(o).wait_send()
        sum_out(o).wait_send()

    @pl.when(f < nf - 1)
    def _():
        halo_next().wait_send()

    @pl.when(f > 0)
    def _():
        halo_prev(0).wait_send()
        halo_prev(1).wait_send()

    for i in range(4):
        copy_w(i).wait_send()
    for h in range(2):
        for sgn in (1, -1):

            @pl.when(valid(z + sgn))
            def _():
                copy_z(z, h, sgn).wait_send()

    def sent(zz):
        for h in range(2):
            copy_x(zz, h).wait_send()
            copy_c(zz, h, 0).wait_send()
            copy_c(zz, h, 1).wait_send()

    def drain(zz, sgn):
        for h in range(2):

            @pl.when(valid(z - sgn))
            def _():
                copy_z(zz, h, -sgn).wait_send()

            result_own(zz, h).wait_send()
            result_near(zz, h).wait_send()

        sent(zz)

    sent(z)
    for s in range(1, nz):
        around(s, drain)


def fused(nf, nt, dout, w_out, y_scan, z_gate, x_conv, du_scan, conv_w, conv_b):
    tok, depth = dout.shape
    rows = w_out.shape[0]
    width = x_conv.shape[1]
    nz = nf // 2
    wide = width // nf
    anywhere = pl.BlockSpec(memory_space=pltpu.HBM)
    vmem = pl.BlockSpec(memory_space=pltpu.VMEM)
    dma = pltpu.SemaphoreType.DMA
    grad_y, grad_z, grad_x, grad_w, grad_b = pl.pallas_call(
        functools.partial(kernel, nf, nt),
        out_shape=[jax.ShapeDtypeStruct((tok, width), BF16)] * 3 + [jax.ShapeDtypeStruct((KW, width), F32), jax.ShapeDtypeStruct((1, width), F32)],
        in_specs=[anywhere] * 6 + [vmem] * 2,
        out_specs=[vmem] * 5,
        scratch_shapes=[
            pltpu.VMEM((nz, nt, 2, tok // 2, depth), BF16),
            pltpu.VMEM((rows, nt * depth), BF16),
            pltpu.VMEM((2, rows // 2, nt * depth), BF16),
            pltpu.VMEM((nt, depth, rows), BF16),
            pltpu.VMEM((nt, depth, rows // 2), BF16),
            pltpu.VMEM((nz, 2, 4, tok // 2, rows // 2), F32),
            pltpu.VMEM((nf, 2, 2, tok // 2, rows // 2), F32),
            pltpu.VMEM((tok, width), BF16),
            pltpu.VMEM((tok, width), BF16),
            pltpu.VMEM((tok, width), BF16),
            pltpu.VMEM((tok, width), BF16),
            pltpu.VMEM((HALO, width), BF16),
            pltpu.VMEM((2, HALO, width), BF16),
            pltpu.VMEM((tok + 16, wide), F32),
            pltpu.VMEM((tok + 8, wide), F32),
            pltpu.VMEM((tok + 8, wide), F32),
            pltpu.VMEM((nf, 8, wide), F32),
            pltpu.VMEM((nf, 8, wide), F32),
            pltpu.VMEM((nf, 8, wide), F32),
            dma((7,)),
            dma((nz, nt, 2)),
            dma((nz, 2, 2)),
            dma((nz, 2)),
            dma((nz, 2, 2)),
            dma((4,)),
            dma((4,)),
            dma((nz, 4)),
            dma((nf, 2)),
            dma((3,)),
            dma((3,)),
            dma((nf,)),
            dma((nf,)),
            dma((nf,)),
            dma((nf,)),
        ],
        compiler_params=pltpu.CompilerParams(
            collective_id=0, has_side_effects=True, vmem_limit_bytes=52 * 1024 * 1024
        ),
    )(dout, w_out, y_scan, z_gate, x_conv, du_scan, conv_w, conv_b[None, :])
    return grad_y, grad_z, grad_x, grad_w, grad_b[0]


def shifted(block, axis, distance):
    devices = range(lax.axis_size(axis))
    route = [(i - distance, i) for i in devices if i - distance in devices]
    return lax.ppermute(block, axis, route)


def gathered(dout, w_out, y_scan, z_gate, x_conv, du_scan, conv_w, conv_b):
    tok_rows = x_conv.shape[0]
    width = x_conv.shape[1]
    prior = shifted(x_conv[tok_rows - (KW - 1) :], "fsdp", 1)
    leading = jnp.stack([x_conv[: KW - 1], du_scan[: KW - 1]])
    later = shifted(leading, "fsdp", -1)
    extended = jnp.concatenate([prior, x_conv, later[0]], 0)
    span = tok_rows + KW - 1
    pre_all = jnp.zeros((span, width), F32) + conv_b[None, :]
    for k in range(KW):
        pre_all = pre_all + conv_w[k][None, :] * extended[k : k + span]
    arriving = jnp.concatenate([du_scan, later[1]], 0)
    d_pre_all = arriving.astype(F32) * silu_slope(pre_all)
    d_pre = d_pre_all[:tok_rows]
    grad_x = jnp.zeros((tok_rows, width), F32)
    taps = []
    for k in range(KW):
        grad_x = grad_x + conv_w[k][None, :] * d_pre_all[KW - 1 - k : KW - 1 - k + tok_rows]
        taps.append(jnp.sum(d_pre * extended[k : k + tok_rows], 0))
    grad_w, grad_b = lax.psum((jnp.stack(taps), jnp.sum(d_pre, 0)), "fsdp")
    full_out = lax.all_gather(dout, "tp", axis=1, tiled=True)
    group_w = lax.all_gather(w_out, "fsdp", axis=0, tiled=True)
    d_gated = lax.dot_general(
        full_out, group_w, (((1,), (1,)), ((), ())), preferred_element_type=F32
    )
    gate_f = z_gate.astype(F32)
    grad_y = (d_gated * jax.nn.silu(gate_f)).astype(BF16)
    grad_z = (d_gated * y_scan.astype(F32) * silu_slope(gate_f)).astype(BF16)
    return (grad_y, grad_z, grad_x.astype(BF16), grad_w, grad_b)


def solution(mesh):
    nf, nt = mesh.shape["fsdp"], mesh.shape["tp"]

    def local(dout, w_out, *rest):
        rows = w_out.shape[0]
        kept = nf // 2 * nt * dout.size * 2
        fits = nt == 4 and nf % 2 == 0 and nf >= 8 and rows % 256 == 0 and kept <= 16 * 1024 * 1024
        body = functools.partial(fused, nf, nt) if fits else gathered
        return body(dout, w_out, *rest)

    return jax.shard_map(
        local,
        mesh=mesh,
        in_specs=(
            P("fsdp", "tp"),
            P(("tp", "fsdp"), None),
            P("fsdp", "tp"),
            P("fsdp", "tp"),
            P("fsdp", "tp"),
            P("fsdp", "tp"),
            P(None, "tp"),
            P("tp"),
        ),
        out_specs=(P("fsdp", "tp"), P("fsdp", "tp"), P("fsdp", "tp"), P(None, "tp"), P("tp")),
        check_vma=False,
    )
```
